512 devices in a mesh: dp: 64 (over y, z), tensor: 8 (over x, core).
Axes of the slice: x: 4, y: 4, z: 16, core: 2. Of those that a mesh axis runs over, the one named last changes fastest.
Arguments:
- grad_values: bfloat16 [64, 128, 4, 6144], P('dp', None, None, 'tensor'), may hold values from -24 to 24
- grad_scales: float32 [64, 128], P('dp'), may hold values from 0.25 to 4
- owner_ids: int32 [128, 1], replicated, may hold values from 0 to 63; in each aligned block of 128 rows (0 to 127, 128 to 255, ...) at most 4 rows name the same one
- step_count: int32 [1], replicated, may hold values from 1 to 3
- master: bfloat16 [64, 4, 4, 6144], P('dp', None, None, 'tensor'), may hold values from -4 to 4
- moment1: bfloat16 [64, 4, 4, 6144], P('dp', None, None, 'tensor'), may hold values from -0.59765625 to 0.59765625
- moment2: bfloat16 [64, 4, 4, 6144], P('dp', None, None, 'tensor'), may hold values from 0.0049743652 to 0.19921875
Outputs:
- new_master: bfloat16 [64, 4, 4, 6144], P('dp', None, None, 'tensor')
- new_moment1: bfloat16 [64, 4, 4, 6144], P('dp', None, None, 'tensor')
- new_moment2: bfloat16 [64, 4, 4, 6144], P('dp', None, None, 'tensor')
- quantized: bfloat16 [128, 4, 6144], P(None, None, 'tensor')
- weight_scales: float32 [128], replicated
The draws below stay inside these ranges and needn't reach their ends.
Inputs may be any that keep to these rules, and one draw needn't show every extreme that they name: `owner_ids`: each of the 64 owners holds 1 to 4 tensors, and some owner holds exactly 4.
All inputs are finite; a program needn't handle non-finite values. Where the reference program divides by a largest or mean magnitude, that divisor is 1e-20 or more.
Results may differ from the reference program's by a relative error of at most 0.015.
Values may be sent and summed in bfloat16 or wider, within the bound.
A program may use at most 64 MiB of HBM per device.

```python
import math
import jax
import jax.numpy as jnp
import numpy as np
from jax import lax

D = 6144
R = 4
SLOTS = 4
NT = 128
N_DP = 64


def log_spread(key, count, lower, upper):
    return jnp.exp(jax.random.uniform(key, (count,), jnp.float32, math.log(lower), math.log(upper)))


def draw_grad_values(key, part):
    key = jax.random.fold_in(key, 11)
    level_key, column_key, noise_key = jax.random.split(key, 3)
    ramp = jnp.exp(math.log(3.0) * (jnp.arange(D, dtype=jnp.float32) / float(max(D - 1, 1)) - 0.5))
    columns = ramp * log_spread(column_key, D, 0.5, 2.0)
    noise = jax.random.truncated_normal(noise_key, -3.0, 3.0, (N_DP, NT, R, D), jnp.float32)
    levels = log_spread(level_key, NT, 0.1, 3.0)
    base = noise
    values = base * levels[None, :, None, None] * columns[None, None, None, :]
    return jnp.clip(values, -24.0, 24.0).astype(jnp.bfloat16)


def shard_levels(own_key, shape, cuts, low, largest):
    factor_of, own = 1.0, jax.random.fold_in(own_key, 6)
    for axis_at, blocks in cuts:
        steps = jnp.exp(jax.random.uniform(jax.random.fold_in(own, axis_at), (blocks,), jnp.float32, low / len(cuts), largest / len(cuts)))
        factor_of = factor_of * jnp.repeat(steps, shape[axis_at] // blocks).reshape([-1 if axis == axis_at else 1 for axis in range(len(shape))])
    return factor_of


def assign_block(stream_key, own, number, rows, number_of, top, reach, skew):
    order = jax.random.permutation(stream_key, number_of)
    crowded, common = portions_of(number_of, rows * top, reach, skew, True), portions_of(number_of, rows * top, reach, skew, False)
    places = jnp.arange(number_of)

    def named(lengths, offset_by):
        used = int((lengths > 0).sum())
        fixed = max(1, used // 4)
        shifted = fixed + (places - fixed + offset_by * (used - fixed)) % max(1, number_of - fixed)
        return jnp.zeros((number_of,), jnp.int32).at[order[jnp.where(places < fixed, places, shifted)]].set(jnp.asarray(lengths, jnp.int32))

    lengths = jnp.where(number % 4 == 0, named(crowded, number // 4), named(common, number - number // 4 - 1))
    mixed = jax.random.permutation(jax.random.fold_in(own, 3), number_of)
    giver, sink = mixed[0:number_of // 2 * 2:2], mixed[1:number_of // 2 * 2:2]
    slack = jnp.minimum(lengths[giver] - 1, reach - lengths[sink]) // 2
    slack = jnp.where((giver == order[0]) | (sink == order[0]) | (lengths[sink] == 0), 0, jnp.maximum(slack, 0))
    shifted = jax.random.randint(jax.random.fold_in(own, 4), (number_of // 2,), 0, 1 << 20) % (slack + 1)
    lengths = lengths.at[giver].add(-shifted).at[sink].add(shifted)
    labels = jnp.searchsorted(jnp.cumsum(lengths), jnp.arange(rows * top), side="right").astype(jnp.int32)
    listing = labels.reshape(top, rows).T
    listing = listing[jax.random.permutation(jax.random.fold_in(own, 1), rows)]
    offset_by = jax.random.randint(jax.random.fold_in(own, 2), (rows, 1), 0, top)
    return jnp.take_along_axis(listing, (jnp.arange(top)[None, :] + offset_by) % top, axis=1)


def portions_of(number_of, total, most, slope, full):
    weights = [(1 << 20) // math.isqrt(grade ** slope) + 1 for grade in range(1, number_of + 1)]
    largest = most if full else min(most, max(-(-total // number_of), total * weights[0] // sum(weights)))
    least = 1 if total - largest >= number_of - 1 else 0
    holding, surplus = [largest] + [least] * (number_of - 1), total - largest - least * (number_of - 1)
    while surplus > 0:
        free = [i for i in range(1, number_of) if holding[i] < largest] or [i for i in range(1, number_of) if holding[i] < most]
        mass, remaining = sum([weights[i] for i in free]), surplus
        for i in free:
            more = min(most - holding[i], max(1, remaining * weights[i] // mass), surplus)
            holding[i] = holding[i] + more
            surplus = surplus - more
    return np.array(holding)


def normal_values(own_key, dims, deviation, reach, shards=(), kind=jnp.bfloat16):
    values = jax.random.normal(own_key, dims, jnp.float32) * deviation
    if len(shards) > 0:
        values = shard_levels(own_key, dims, shards, -0.22, 0.18) * values
    return jnp.clip(values, min=-reach, max=reach).astype(kind)


def setup_inputs(seed: int = 0) -> dict:
    key_list = jax.random.split(jax.random.key(seed), 8)
    grad_values = draw_grad_values(jax.random.fold_in(key_list[7], 71), 0)
    grad_scales = jnp.clip(jnp.exp(math.log(4.0) - 2.7725887 * jax.random.uniform(key_list[1], (N_DP, NT), jnp.float32) ** shard_levels(key_list[1], (N_DP, NT), ((0, 64),), -0.2, 0.2)), 0.25, 4.0)
    owner_ids_keys = jax.random.split(jax.random.fold_in(key_list[2], 1), NT // NT)
    owner_ids_turns = jax.random.permutation(jax.random.fold_in(key_list[2], 3), NT // NT)
    owner_ids = jax.vmap(lambda own, number: assign_block(jax.random.fold_in(key_list[2], 2), own, number, NT, N_DP, 1, SLOTS, 2))(owner_ids_keys, owner_ids_turns).reshape((NT, 1))
    step_count = jax.random.randint(key_list[3], (1,), 1, 4).astype(jnp.int32)
    master = normal_values(key_list[4], (N_DP, SLOTS, R, D), 1.0, 4.0, ((0, 64), (3, 8)))
    moment1 = normal_values(key_list[5], (N_DP, SLOTS, R, D), 0.1, 0.59765625, ((0, 64), (3, 8)))
    moment2 = jnp.clip(jnp.exp(math.log(0.19921875) - 3.6901057 * jax.random.uniform(key_list[6], (N_DP, SLOTS, R, D), jnp.float32) ** shard_levels(key_list[6], (N_DP, SLOTS, R, D), ((0, 64), (3, 8)), -0.2, 0.2)), 0.0049743652, 0.19921875).astype(jnp.bfloat16)
    return dict(grad_values=grad_values, grad_scales=grad_scales, owner_ids=owner_ids, step_count=step_count, master=master, moment1=moment1, moment2=moment2)


BETA_ONE = 0.9
BETA_TWO = 0.95
RATE = 0.1
DECAY = 0.1
ADAM_EPS = 1e-08
PEAK_EPS = 1e-06
CLIP_RMS = 0.5

def slot_ranks(owner_list):
    count = owner_list.shape[0]
    same = (owner_list[:, None] == owner_list[None, :]).astype(jnp.int32)
    earlier = (jnp.arange(count)[None, :] < jnp.arange(count)[:, None]).astype(jnp.int32)
    return lax.optimization_barrier(jnp.sum(same * earlier, axis=1)).astype(jnp.int32)

def adam_update(summed, factor, step_count, master, moment1, moment2):
    step_value = step_count[0].astype(jnp.float32)
    clipped = summed * factor
    first = BETA_ONE * moment1.astype(jnp.float32) + (1.0 - BETA_ONE) * clipped
    second = BETA_TWO * moment2.astype(jnp.float32) + (1.0 - BETA_TWO) * clipped * clipped
    first_hat = first / (1.0 - jnp.power(jnp.float32(BETA_ONE), step_value))
    second_hat = second / (1.0 - jnp.power(jnp.float32(BETA_TWO), step_value))
    weight = master.astype(jnp.float32)
    updated = weight - RATE * (first_hat / (jnp.sqrt(second_hat) + ADAM_EPS) + DECAY * weight)
    return (updated.astype(jnp.bfloat16), first.astype(jnp.bfloat16), second.astype(jnp.bfloat16))

def reference(grad_values, grad_scales, owner_ids, step_count, master, moment1, moment2):
    owner_list = owner_ids[:, 0]

    def add_replica(replica, total):
        values = lax.dynamic_index_in_dim(grad_values, replica, 0, keepdims=False).astype(jnp.float32)
        scales = lax.dynamic_index_in_dim(grad_scales, replica, 0, keepdims=False)
        return total + values * scales[:, None, None]
    total = lax.fori_loop(0, N_DP, add_replica, jnp.zeros((NT, R, D), jnp.float32))
    squares = jnp.sum(total * total)
    factor = jnp.minimum(1.0, CLIP_RMS * jnp.sqrt(jnp.float32(NT * R * D)) / jnp.sqrt(squares + 1e-06))
    slot_of = slot_ranks(owner_list)
    positions = (owner_list * SLOTS + slot_of).astype(jnp.int32)
    flat_master = master.reshape(N_DP * SLOTS, R, D)
    flat_first = moment1.reshape(N_DP * SLOTS, R, D)
    flat_second = moment2.reshape(N_DP * SLOTS, R, D)
    summed = jnp.zeros((N_DP * SLOTS, R, D), jnp.float32).at[positions].set(total)
    live_slots = jnp.zeros((N_DP * SLOTS,), jnp.int32).at[positions].set(1) > 0
    new_w, new_m, new_v = adam_update(summed, factor, step_count, flat_master, flat_first, flat_second)
    keep = live_slots[:, None, None]
    new_w = jnp.where(keep, new_w, flat_master)
    new_m = jnp.where(keep, new_m, flat_first)
    new_v = jnp.where(keep, new_v, flat_second)
    slot_peak = lax.optimization_barrier(jnp.max(jnp.abs(new_w.astype(jnp.float32)), axis=(1, 2))) + PEAK_EPS
    scaled_all = (new_w.astype(jnp.float32) / slot_peak[:, None, None]).astype(jnp.bfloat16)
    quantized = scaled_all[positions]
    weight_scales = slot_peak[positions]
    shape_out = (N_DP, SLOTS, R, D)
    return (new_w.reshape(shape_out), new_m.reshape(shape_out), new_v.reshape(shape_out), quantized, weight_scales)
```

```python
import jax
import jax.numpy as jnp
from jax import lax
from jax.experimental import pallas as pl
from jax.experimental.pallas import tpu as pltpu
from jax.sharding import PartitionSpec as P

BETA_ONE = 0.9
BETA_TWO = 0.95
RATE = 0.1
DECAY = 0.1
ADAM_EPS = 1e-08
PEAK_EPS = 1e-06
CLIP_RMS = 0.5

NY, NZ, NX, NC = 4, 16, 4, 2
NT, SLOTS, R, COLS = 128, 4, 4, 768
CB = COLS // 128
BLKS = CB * R
E = BLKS * 128
YE = E // NY
PER = YE // NZ
YB = BLKS // NY
MESH = pl.DeviceIdType.MESH
BF, F32 = jnp.bfloat16, jnp.float32

_counts = dict(
    sy=3, sz=15, gy=48, gz=15, qz=15, qy=3, qt=7, dz=15, dy=3, az=15, ay=48, mz=15, my=3, mt=7
)
BASE, _total = {}, 0
for _name, _count in _counts.items():
    BASE[_name] = _total
    _total += _count


def offset_of(j):
    return 8 + (1 - 2 * (j % 2)) * ((j + 1) // 2)


def adam(g, step, master, first, second):
    m = BETA_ONE * first + (1.0 - BETA_ONE) * g
    v = BETA_TWO * second + (1.0 - BETA_TWO) * g * g
    one = 1.0 - jnp.exp(step * jnp.log(jnp.full_like(step, BETA_ONE)))
    two = 1.0 - jnp.exp(step * jnp.log(jnp.full_like(step, BETA_TWO)))
    m_hat = m / one
    v_hat = v / two
    w = master - RATE * (m_hat / (jnp.sqrt(v_hat) + ADAM_EPS) + DECAY * master)
    return w, m, v


def kernel(
    g_ref, gs_ref, own_ref, step_ref, w_ref, m_ref, v_ref,
    nw_ref, nm_ref, nv_ref, quant_ref, scale_ref,
    gv, fs, tv, sv, sf, ysf, ys, syr, st, szs, szr,
    yr, zs, zr, sbp, dsend, dr, dys, dyr, s2, nv,
    qsend, qzr, qys, qyr, qts, qtr,
    msend, mzr, mys, myr, mts, mtr,
    wown, agb, ov,
    lsem, ssem, rsem,
):
    dp, tp = lax.axis_index("dp"), lax.axis_index("tensor")
    y, z = dp // NZ, dp % NZ

    def at_z(zz):
        return (y * NZ + zz, tp)

    def at_y(yy):
        return (yy * NZ + z, tp)

    def at_t(tt):
        return (dp, tt)

    def send(kind, i, src, dst, dev):
        pltpu.make_async_remote_copy(
            src_ref=src, dst_ref=dst, send_sem=ssem.at[BASE[kind] + i],
            recv_sem=rsem.at[BASE[kind] + i], device_id=dev, device_id_type=MESH,
        ).start()

    def arrived(kind, i, ref):
        pltpu.make_async_copy(ref, ref, rsem.at[BASE[kind] + i]).wait()

    def sent(kind, count, ref):
        def body(i, carry):
            pltpu.make_async_copy(ref, ref, ssem.at[BASE[kind] + i]).wait()
            return carry
        lax.fori_loop(0, count, body, 0)

    state = (w_ref, m_ref, v_ref)

    def g_copy(cb):
        return pltpu.make_async_copy(g_ref.at[:, :, pl.ds(cb * 128, 128)], gv.at[cb], lsem.at[cb])

    def s_copy(a, cb):
        return pltpu.make_async_copy(
            state[a].at[:, :, pl.ds(cb * 128, 128)], sv.at[a, cb], lsem.at[CB + a * CB + cb]
        )

    for cb in range(CB):
        g_copy(cb).start()
    for a in range(3):
        for cb in range(CB):
            s_copy(a, cb).start()

    barrier = pltpu.get_barrier_semaphore()

    def greet(peers, device_of):
        def body(k, carry):
            pl.semaphore_signal(barrier, inc=1, device_id=device_of(k), device_id_type=MESH)
            return carry
        lax.fori_loop(1, peers, body, 0)

    greet(NZ, lambda k: at_z((z + k) % NZ))
    greet(NY, lambda k: at_y((y + k) % NY))
    greet(NX * NC, lambda k: at_t((tp + k) % (NX * NC)))

    scales = gs_ref[...]
    g2 = gv.reshape(CB, NT * R, 128)
    for cb in range(CB):
        g_copy(cb).wait()
        fs[...] = g2[cb].astype(F32)
        for r in range(R):
            block = fs[pl.ds(r, NT, stride=R), :]
            tv[pl.ds((cb * R + r) * 128, 128), :] = (block.T * scales).astype(BF)

    for a in range(3):
        for cb in range(CB):
            s_copy(a, cb).wait()
    sf[...] = sv.reshape(3 * CB * SLOTS * R, 128)[...].astype(F32)
    ysf[...] = jnp.zeros_like(ysf)
    for a in range(3):
        for r in range(R):
            rows = sf[pl.ds(a * CB * SLOTS * R + r, CB * SLOTS, stride=R), :]
            ysf[:, pl.ds(r * 16 + a * 4, 4), :] = rows.reshape(CB, SLOTS, 128)
    ys[...] = ysf[...].reshape(NY, YB * 16, 128).astype(BF)

    pl.semaphore_wait(barrier, (NZ - 1) + (NY - 1) + (NX * NC - 1))

    for k in range(1, NY):
        yy = (y + k) % NY
        send("sy", k - 1, ys.at[yy], syr.at[y], at_y(yy))

    def y_send(j, carry):
        zz = (z + offset_of(j)) % NZ
        for k in range(1, NY):
            yy = (y + k) % NY
            src = tv.at[pl.ds(pl.multiple_of((yy * NZ + zz) * PER, 16), PER)]
            send("gy", j * 3 + k - 1, src, yr.at[j, k - 1], at_y(yy))
        return carry

    lax.fori_loop(0, NZ, y_send, 0)

    def y_sum(j):
        zz = (z + offset_of(j)) % NZ
        total = tv[pl.ds(pl.multiple_of((y * NZ + zz) * PER, 16), PER), :].astype(F32)
        for k in range(3):
            arrived("gy", j * 3 + k, yr.at[j, k])
            total = total + yr[j, k].astype(F32)
        return total

    def z_send(j, carry):
        zz = (z + offset_of(j)) % NZ
        zs[j] = y_sum(j).astype(BF)
        send("gz", j, zs.at[j], zr.at[j], at_z(zz))
        return carry

    lax.fori_loop(0, NZ - 1, z_send, 0)
    mine = y_sum(NZ - 1)

    syr[y] = ys[y]
    for k in range(1, NY):
        arrived("sy", k - 1, syr.at[(y - k + NY) % NY])
    for b in range(YB):
        block = syr[:, pl.ds(b * 16, 16), :].reshape(NY * 16, 128).astype(F32)
        block = jnp.concatenate([block, jnp.zeros((128 - NY * 16, 128), F32)], axis=0)
        st[pl.ds(b * 128, 128), :] = block.T
    for zz in range(NZ):
        upper = st[pl.ds(zz * PER, 16), :] + pltpu.roll(st[pl.ds(zz * PER + 16, 16), :], 64, 1)
        szs[zz, pl.ds(0, 16), :] = upper.astype(BF)
        szs[zz, pl.ds(16, 16), :] = st[pl.ds(zz * PER + 32, 16), :].astype(BF)

    def sz_send(j, carry):
        zz = (z + offset_of(j)) % NZ
        send("sz", j, szs.at[zz], szr.at[z], at_z(zz))
        return carry

    lax.fori_loop(0, NZ - 1, sz_send, 0)
    szr[z] = szs[z]

    own = own_ref[...]
    spread = jnp.broadcast_to(own.astype(F32), (NT, NT))
    same = spread == spread.T
    before = lax.broadcasted_iota(jnp.int32, (NT, NT), 0) < lax.broadcasted_iota(jnp.int32, (NT, NT), 1)
    slot = jnp.sum(jnp.where(same & before, 1.0, 0.0), axis=0, keepdims=True).astype(jnp.int32)
    own_z, own_y = own & (NZ - 1), own >> 4
    count = jnp.sum(jnp.where(own == dp, 1.0, 0.0), axis=1, keepdims=True)
    place = own_z * 16 + own_y * 4 + slot
    hot = jnp.where(
        lax.broadcasted_iota(jnp.int32, (NZ * 16, NT), 0) == place, 1.0, 0.0
    ).astype(BF)

    def z_add(j, total):
        arrived("gz", j, zr.at[j])
        return total + zr[j].astype(F32)

    summed = lax.fori_loop(0, NZ - 1, z_add, mine)

    def z_stage(kind, value, sendbuf, buf):
        sendbuf[...] = value
        buf[z] = value

        def body(j, carry):
            send(kind, j, sendbuf, buf.at[z], at_z((z + offset_of(j)) % NZ))
            return carry

        lax.fori_loop(0, NZ - 1, body, 0)

    def z_wait(kind, buf):
        def body(j, carry):
            arrived(kind, j, buf.at[(z - offset_of(j) + NZ) % NZ])
            return carry

        lax.fori_loop(0, NZ - 1, body, 0)

    def y_stage(kind, value, sendbuf, buf):
        sendbuf[...] = value
        buf[y] = value
        for k in (2, 1, 3):
            send(kind, k - 1, sendbuf, buf.at[y], at_y((y + k) % NY))

    def y_wait(kind, buf):
        for k in range(1, NY):
            arrived(kind, k - 1, buf.at[(y - k + NY) % NY])

    def t_stage(kind, value, sendbuf, buf):
        sendbuf[...] = value
        buf[tp] = value
        for k in (4, 5, 3, 2, 6, 7, 1):
            send(kind, k - 1, sendbuf, buf.at[tp], at_t((tp + k) % (NX * NC)))

    def t_wait(kind, buf):
        for k in range(1, NX * NC):
            arrived(kind, k - 1, buf.at[(tp - k + NX * NC) % (NX * NC)])

    squares = jnp.sum((summed * summed).reshape(PER // 8, 8, 128), axis=0)
    z_stage("qz", squares, qsend, qzr)

    sum_bf = summed.astype(BF)
    sbp[...] = jnp.zeros_like(sbp)
    sbp[pl.ds(0, PER), :] = sum_bf
    dsend[...] = (
        lax.dot_general(hot, sbp[...], (((1,), (1,)), ((), ())), preferred_element_type=F32)
        .astype(BF)
        .reshape(NZ, 16, 128)
    )

    def d_send(j, carry):
        zz = (z + offset_of(j)) % NZ
        send("dz", j, dsend.at[zz], dr.at[z], at_z(zz))
        return carry

    lax.fori_loop(0, NZ - 1, d_send, 0)
    dr[z] = dsend[z]

    z_wait("sz", szr)
    low = lax.broadcasted_iota(jnp.int32, (16, 128), 1) < 64
    parts = [[], [], []]
    for pair in range(NZ // 2):
        even0, even1 = szr[2 * pair, pl.ds(0, 16), :].astype(F32), szr[2 * pair, pl.ds(16, 16), :].astype(F32)
        odd0, odd1 = szr[2 * pair + 1, pl.ds(0, 16), :].astype(F32), szr[2 * pair + 1, pl.ds(16, 16), :].astype(F32)
        parts[0].append(jnp.where(low, even0, pltpu.roll(odd0, 64, 1)))
        parts[1].append(jnp.where(low, pltpu.roll(even0, 64, 1), odd0))
        parts[2].append(jnp.where(low, even1, pltpu.roll(odd1, 64, 1)))
    packed = jnp.concatenate([jnp.concatenate(p, axis=1) for p in parts], axis=0).astype(BF)
    target = own_z * 64 + own_y * 16 + slot
    rows = lax.broadcasted_iota(jnp.int32, (NZ * 64, NT), 0)
    old = []
    for a in range(3):
        pick = jnp.where(rows == target + 4 * a, 1.0, 0.0).astype(BF)
        old.append(jnp.dot(packed, pick, preferred_element_type=F32))

    z_wait("qz", qzr)
    y_stage("qy", jnp.sum(qzr[...], axis=0), qys, qyr)
    y_wait("qy", qyr)
    t_stage("qt", jnp.sum(qyr[...], axis=0), qts, qtr)
    t_wait("qt", qtr)
    all_squares = jnp.sum(jnp.sum(qtr[...], axis=0), axis=(0, 1), keepdims=True)
    entries = float(NT * R * COLS * NX * NC)
    factor = jnp.minimum(
        1.0, CLIP_RMS * jnp.sqrt(jnp.full((1, 1), entries, F32)) / jnp.sqrt(all_squares + 1e-06)
    )
    step = jnp.full((1, 1), step_ref[0].astype(F32), F32)

    new_w, _, _ = adam(sum_bf.astype(F32) * factor, step, old[0], old[1], old[2])
    new_w = new_w.astype(BF)
    here = pl.multiple_of(dp * PER, 16)
    wown[...] = new_w
    agb[pl.ds(here, PER), :] = new_w

    def slice_at(ref, yy, zz):
        return ref.at[pl.ds(pl.multiple_of((yy * NZ + zz) * PER, 16), PER)]

    def a_send(j, carry):
        send("az", j, wown, slice_at(agb, y, z), at_z((z + offset_of(j)) % NZ))
        return carry

    lax.fori_loop(0, NZ - 1, a_send, 0)
    for k in range(1, NY):
        send("ay", (NZ - 1) * 3 + k - 1, wown, slice_at(agb, y, z), at_y((y + k) % NY))
    peak = jnp.max(jnp.abs(new_w.astype(F32)).reshape(PER // 8, 8, 128), axis=0)
    z_stage("mz", peak, msend, mzr)

    def a_forward(i, carry):
        j = NZ - 2 - i
        zz = (z - offset_of(j) + NZ) % NZ
        ref = slice_at(agb, y, zz)
        arrived("az", j, ref)
        for k in range(1, NY):
            send("ay", j * 3 + k - 1, ref, ref, at_y((y + k) % NY))
        return carry

    lax.fori_loop(0, NZ - 1, a_forward, 0)
    z_wait("mz", mzr)
    y_stage("my", jnp.max(mzr[...], axis=0), mys, myr)

    z_wait("dz", dr)
    lane = lax.broadcasted_iota(jnp.int32, (16, 128), 1)
    for b in range(YB):
        block = jnp.zeros((16, 128), F32)
        for zz in range(NZ):
            start = zz * PER - b * 128
            if -PER < start < 128:
                piece = dr[zz].astype(F32)
                if start % 128:
                    piece = pltpu.roll(piece, start % 128, 1)
                if start < 0:
                    piece = jnp.where(lane < start + PER, piece, 0.0)
                elif start + PER > 128:
                    piece = jnp.where(lane >= start, piece, 0.0)
                block = block + piece
        dys[:, pl.ds(b * 4, 4), :] = block.reshape(NY, SLOTS, 128)
    for k in range(1, NY):
        yy = (y + k) % NY
        send("dy", k - 1, dys.at[yy], dyr.at[y], at_y(yy))
    dyr[y] = dys[y]

    y_wait("my", myr)
    t_stage("mt", jnp.max(myr[...], axis=0), mts, mtr)

    y_wait("dy", dyr)
    flat = dyr.reshape(NY * YB * SLOTS, 128)
    for s in range(SLOTS):
        rows_s = flat[pl.ds(s, BLKS, stride=SLOTS), :]
        s2[:, pl.ds(s * R, R), :] = rows_s.reshape(CB, R, 128)
    sums = s2[...].reshape(CB * SLOTS * R, 128)
    size = CB * SLOTS * R
    olds = [sf[pl.ds(a * size, size), :] for a in range(3)]
    news = adam(sums * factor, step, *olds)
    slot_row = (lax.broadcasted_iota(jnp.int32, (size, 128), 0) // R) % SLOTS
    live = slot_row.astype(F32) < count
    nv2 = nv.reshape(3, size, 128)
    outs = (nw_ref, nm_ref, nv_ref)

    def o_copy(a, cb):
        return pltpu.make_async_copy(
            nv.at[a, cb], outs[a].at[:, :, pl.ds(cb * 128, 128)], lsem.at[CB + a * CB + cb]
        )

    for a in range(3):
        nv2[a] = jnp.where(live, news[a], olds[a]).astype(BF)
        for cb in range(CB):
            o_copy(a, cb).start()

    def a_wait(i, carry):
        j = NZ - 1 - i
        zz = (z - offset_of(j) + NZ) % NZ
        for k in range(1, NY):
            arrived("ay", j * 3 + k - 1, slice_at(agb, (y - k + NY) % NY, zz))
        return carry

    lax.fori_loop(0, NZ, a_wait, 0)
    t_wait("mt", mtr)
    peaks = jnp.max(jnp.max(mtr[...], axis=0), axis=0, keepdims=True) + PEAK_EPS
    scale_ref[...] = peaks
    inverse = 1.0 / peaks

    o2 = ov.reshape(CB, NT * R, 128)

    def q_copy(cb):
        return pltpu.make_async_copy(ov.at[cb], quant_ref.at[:, :, pl.ds(cb * 128, 128)], lsem.at[cb])

    for cb in range(CB):
        for r in range(R):
            block = agb[pl.ds((cb * R + r) * 128, 128), :].astype(F32) * inverse
            fs[pl.ds(r, NT, stride=R), :] = block.T
        o2[cb] = fs[...].astype(BF)
        q_copy(cb).start()

    sent("sy", 3, ys.at[0])
    sent("sz", 15, szs.at[0])
    sent("gy", 48, yr.at[0, 0])
    sent("gz", 15, zs.at[0])
    sent("qz", 15, qsend)
    sent("qy", 3, qys)
    sent("qt", 7, qts)
    sent("dz", 15, dsend.at[0])
    sent("dy", 3, dys.at[0])
    sent("az", 15, wown)
    sent("ay", 48, wown)
    sent("mz", 15, msend)
    sent("my", 3, mys)
    sent("mt", 7, mts)
    for a in range(3):
        for cb in range(CB):
            o_copy(a, cb).wait()
    for cb in range(CB):
        q_copy(cb).wait()


def local(grad_values, grad_scales, owner_ids, step_count, master, moment1, moment2):
    vmem = pl.BlockSpec(memory_space=pltpu.VMEM)
    smem = pl.BlockSpec(memory_space=pltpu.SMEM)
    anym = pl.BlockSpec(memory_space=pl.ANY)
    owned = jax.ShapeDtypeStruct((SLOTS, R, COLS), BF)
    V = pltpu.VMEM
    small = lambda n: V((n, 8, 128), F32)
    one = V((8, 128), F32)
    exchange = [one, small(NZ), one, small(NY), one, small(NX * NC)]
    out = pl.pallas_call(
        kernel,
        out_shape=(
            owned, owned, owned,
            jax.ShapeDtypeStruct((NT, R, COLS), BF),
            jax.ShapeDtypeStruct((1, NT), F32),
        ),
        in_specs=[anym, vmem, vmem, smem, anym, anym, anym],
        out_specs=(anym, anym, anym, anym, vmem),
        scratch_shapes=[
            V((CB, NT, R, 128), BF),
            V((NT * R, 128), F32),
            V((E, NT), BF),
            V((3, CB, SLOTS, R, 128), BF),
            V((3 * CB * SLOTS * R, 128), F32),
            V((CB, R * 16, 128), F32),
            V((NY, YB * 16, 128), BF),
            V((NY, YB * 16, 128), BF),
            V((YE, 128), F32),
            V((NZ, 32, 128), BF),
            V((NZ, 32, 128), BF),
            V((NZ, 3, PER, NT), BF),
            V((NZ, PER, NT), BF),
            V((NZ, PER, NT), BF),
            V((128, NT), BF),
            V((NZ, 16, 128), BF),
            V((NZ, 16, 128), BF),
            V((NY, YB * SLOTS, 128), F32),
            V((NY, YB * SLOTS, 128), F32),
            V((CB, SLOTS * R, 128), F32),
            V((3, CB, SLOTS, R, 128), BF),
        ]
        + exchange
        + exchange
        + [
            V((PER, NT), BF),
            V((E, NT), BF),
            V((CB, NT, R, 128), BF),
            pltpu.SemaphoreType.DMA((4 * CB,)),
            pltpu.SemaphoreType.DMA((_total,)),
            pltpu.SemaphoreType.DMA((_total,)),
        ],
        compiler_params=pltpu.CompilerParams(
            collective_id=0, has_side_effects=True, vmem_limit_bytes=40 << 20
        ),
    )(
        grad_values[0], grad_scales, owner_ids.reshape(1, NT), step_count,
        master[0], moment1[0], moment2[0],
    )
    return out[0][None], out[1][None], out[2][None], out[3], out[4].reshape(NT)


def solution(mesh):
    split = P("dp", None, None, "tensor")
    return jax.shard_map(
        local,
        mesh=mesh,
        in_specs=(split, P("dp", None), P(), P(), split, split, split),
        out_specs=(split, split, split, P(None, None, "tensor"), P()),
        check_vma=False,
    )
```

```python
import jax
import jax.numpy as jnp
from jax import lax
from jax.experimental import pallas as pl
from jax.experimental.pallas import tpu as pltpu
from jax.sharding import PartitionSpec as P

BETA_ONE = 0.9
BETA_TWO = 0.95
RATE = 0.1
DECAY = 0.1
ADAM_EPS = 1e-08
PEAK_EPS = 1e-06
CLIP_RMS = 0.5

NY, NZ, NX, NC = 4, 16, 4, 2
NT, SLOTS, R, COLS = 128, 4, 4, 768
CB = COLS // 128
BLKS = CB * R
E = BLKS * 128
YE = E // NY
PER = YE // NZ
YB = BLKS // NY
MESH = pl.DeviceIdType.MESH
BF, F32 = jnp.bfloat16, jnp.float32

KINDS = ("sy", "sz", "gy", "gz", "qw", "qz", "dz", "dy", "az", "ay", "mw", "mz")
SEND = {name: i for i, name in enumerate(KINDS)}
RECV, _total = {}, 0
for _name in KINDS:
    RECV[_name] = _total
    _total += {"gy": NZ, "gz": 3, "az": NZ}.get(_name, 1)
NW = NY * NX * NC
DIRECT = (8, 4, -4, 2, -2, 1, -1, 0)
SPREAD = (4, -4, 8, 3, -3, 2, -2, 1, -1)


def far_offset(j):
    return 8 + (1 - 2 * (j & 1)) * ((j + 1) >> 1)


def relayed(i):
    p = i >> 1
    return 1 - 2 * (i & 1), 7 - p - (p + 1 >> 2)


def adam(g, step, master, first, second):
    m = BETA_ONE * first + (1.0 - BETA_ONE) * g
    v = BETA_TWO * second + (1.0 - BETA_TWO) * g * g
    one = 1.0 - jnp.exp(step * jnp.log(jnp.full_like(step, BETA_ONE)))
    two = 1.0 - jnp.exp(step * jnp.log(jnp.full_like(step, BETA_TWO)))
    m_hat = m / one
    v_hat = v / two
    w = master - RATE * (m_hat / (jnp.sqrt(v_hat) + ADAM_EPS) + DECAY * master)
    return w, m, v


def kernel(
    g_ref, gs_ref, own_ref, step_ref, w_ref, m_ref, v_ref,
    agb, nv, peak_ref,
    gv, gsv, ownv, stepv, peakv, fs, tv, sv, sf, ysf, ys, syr, st, szs, szr,
    yr, zs, rr, zr, sbp, dsend, dr, dys, dyr, s2, nvs,
    qws, qwr, qzs, qzr, mws, mwr, mzs, mzr,
    wown, zg,
    lsem, ssem, rsem, ready,
):
    dp, tp = lax.axis_index("dp"), lax.axis_index("tensor")
    y, z = dp >> 4, dp & (NZ - 1)
    w_me = y * (NX * NC) + tp

    def at_z(zz):
        return (y * NZ + zz, tp)

    def at_y(yy):
        return (yy * NZ + z, tp)

    def at_w(k):
        return (((y + (k >> 3)) & (NY - 1)) * NZ + z, (tp + k) & (NX * NC - 1))

    def near(d):
        return (z + d + NZ) & (NZ - 1)

    def send(kind, i, src, dst, dev):
        pltpu.make_async_remote_copy(
            src_ref=src, dst_ref=dst, send_sem=ssem.at[SEND[kind]],
            recv_sem=rsem.at[RECV[kind] + i], device_id=dev, device_id_type=MESH,
        ).start()

    def arrived(kind, i, ref):
        pltpu.make_async_copy(ref, ref, rsem.at[RECV[kind] + i]).wait()

    def sent(kind, ref):
        pltpu.make_async_copy(ref, ref, ssem.at[SEND[kind]]).wait()

    barrier = pltpu.get_barrier_semaphore()

    def greet(device):
        pl.semaphore_signal(barrier, inc=1, device_id=device, device_id_type=MESH)

    for d in (4, -4, 3, -3, 2, -2, 1, -1):
        greet(at_z(near(d)))
    for k in (4, 5, 3, 2, 6, 7, 1):
        greet(at_w(k))
    for k in (2, 1, 3):
        greet(at_y((y + k) & (NY - 1)))

    state = (w_ref, m_ref, v_ref)

    def g_copy(cb):
        return pltpu.make_async_copy(g_ref.at[:, :, pl.ds(cb * 128, 128)], gv.at[cb], lsem.at[cb])

    def s_copy(a, cb):
        return pltpu.make_async_copy(
            state[a].at[:, :, pl.ds(cb * 128, 128)], sv.at[a, cb], lsem.at[CB + a * CB + cb]
        )

    gs_copy = pltpu.make_async_copy(gs_ref, gsv, lsem.at[4 * CB])
    own_copy = pltpu.make_async_copy(own_ref, ownv, lsem.at[4 * CB + 1])
    gs_copy.start()
    for cb in range(CB):
        g_copy(cb).start()
    own_copy.start()
    step_copy = pltpu.make_async_copy(step_ref, stepv, lsem.at[4 * CB + 2])
    step_copy.start()
    for a in range(3):
        for cb in range(CB):
            s_copy(a, cb).start()

    gs_copy.wait()
    scales = gsv[...]
    g2 = gv.reshape(CB, NT * R, 128)
    for cb in range(CB):
        g_copy(cb).wait()
        fs[...] = g2[cb].astype(F32)
        for r in range(R):
            block = fs[pl.ds(r, NT, stride=R), :]
            tv[pl.ds((cb * R + r) * 128, 128), :] = (block.T * scales).astype(BF)

    for a in range(3):
        for cb in range(CB):
            s_copy(a, cb).wait()
    sf[...] = sv.reshape(3 * CB * SLOTS * R, 128)[...].astype(F32)
    ysf[...] = jnp.zeros_like(ysf)
    for a in range(3):
        for r in range(R):
            rows = sf[pl.ds(a * CB * SLOTS * R + r, CB * SLOTS, stride=R), :]
            ysf[:, pl.ds(r * 16 + a * 4, 4), :] = rows.reshape(CB, SLOTS, 128)
    ys[...] = ysf[...].reshape(NY, YB * 16, 128).astype(BF)

    pl.semaphore_wait(barrier, 8 + (NX * NC - 1) + (NY - 1))

    for k in range(1, NY):
        yy = (y + k) & (NY - 1)
        send("sy", 0, ys.at[yy], syr.at[y], at_y(yy))
    syr[y] = ys[y]

    def slice_at(ref, yy, zz):
        return ref.at[pl.ds(pl.multiple_of((yy * NZ + zz) * PER, 16), PER)]

    def y_send(i, zz):
        for k in range(1, NY):
            yy = (y + k) & (NY - 1)
            send("gy", i, slice_at(tv, yy, zz), yr.at[i, k - 1], at_y(yy))

    def y_send_relayed(i, carry):
        side, far = relayed(i)
        y_send(i, near(side * far))
        return carry

    lax.fori_loop(0, 8, y_send_relayed, 0)
    for i, d in enumerate(DIRECT):
        y_send(8 + i, near(d))

    for d in (4, -4):
        pl.semaphore_signal(ready, inc=1, device_id=at_z(near(d)), device_id_type=MESH)

    def y_sum(i, zz):
        total = slice_at(tv, y, zz)[...].astype(F32)
        arrived("gy", i, yr.at[i])
        for k in range(3):
            total = total + yr[i, k].astype(F32)
        return total

    def to_relay(i, carry):
        side, far = relayed(i)
        zs[i] = y_sum(i, near(side * far)).astype(BF)
        send("gz", 1 + (i & 1), zs.at[i], rr.at[i & 1, i >> 1], at_z(near(side * (far - 4))))
        return carry

    lax.fori_loop(0, 8, to_relay, 0)
    pl.semaphore_wait(ready, 2)
    for i, d in enumerate(DIRECT[:-1]):
        total = y_sum(8 + i, near(d))
        if abs(d) == 4:
            side = 0 if d > 0 else 1
            arrived("gz", 1 + side, rr.at[side])
            for k in range(4):
                total = total + rr[side, k].astype(F32)
        zs[8 + i] = total.astype(BF)
        send("gz", 0, zs.at[8 + i], zr.at[i], at_z(near(d)))
    mine = y_sum(NZ - 1, z)

    arrived("sy", 0, syr.at[pl.ds(0, NY - 1)])
    for b in range(YB):
        block = syr[:, pl.ds(b * 16, 16), :].reshape(NY * 16, 128).astype(F32)
        block = jnp.concatenate([block, jnp.zeros((128 - NY * 16, 128), F32)], axis=0)
        st[pl.ds(b * 128, 128), :] = block.T
    for zz in range(NZ):
        upper = st[pl.ds(zz * PER, 16), :] + pltpu.roll(st[pl.ds(zz * PER + 16, 16), :], 64, 1)
        szs[zz, pl.ds(0, 16), :] = upper.astype(BF)
        szs[zz, pl.ds(16, 16), :] = st[pl.ds(zz * PER + 32, 16), :].astype(BF)

    own_copy.wait()
    step_copy.wait()
    own = ownv[...]
    spread = jnp.broadcast_to(own.astype(F32), (NT, NT))
    same = spread == spread.T
    before = lax.broadcasted_iota(jnp.int32, (NT, NT), 0) < lax.broadcasted_iota(jnp.int32, (NT, NT), 1)
    slot = jnp.sum(jnp.where(same & before, 1.0, 0.0), axis=0, keepdims=True).astype(jnp.int32)
    own_z, own_y = own & (NZ - 1), own >> 4
    count = jnp.sum(jnp.where(own == dp, 1.0, 0.0), axis=1, keepdims=True)
    place = own_z * 16 + own_y * 4 + slot
    hot = jnp.where(
        lax.broadcasted_iota(jnp.int32, (NZ * 16, NT), 0) == place, 1.0, 0.0
    ).astype(BF)

    arrived("gz", 0, zr)
    summed = mine
    for i in range(len(DIRECT) - 1):
        summed = summed + zr[i].astype(F32)

    def w_stage(kind, value, sendbuf, buf):
        sendbuf[...] = value
        buf[w_me] = value

        def body(i, carry):
            send(kind, 0, sendbuf, buf.at[w_me], at_w(NW - 1 - i))
            return carry

        lax.fori_loop(0, NW - 1, body, 0)

    def w_wait(kind, buf):
        arrived(kind, 0, buf.at[pl.ds(0, NW - 1)])

    def z_stage(kind, value, sendbuf, buf):
        sendbuf[...] = value
        buf[z] = value

        def body(j, carry):
            send(kind, 0, sendbuf, buf.at[z], at_z(near(far_offset(j))))
            return carry

        lax.fori_loop(0, NZ - 1, body, 0)

    def z_wait(kind, buf):
        arrived(kind, 0, buf.at[pl.ds(0, NZ - 1)])

    squares = jnp.sum((summed * summed).reshape(PER // 8, 8, 128), axis=0)
    w_stage("qw", squares, qws, qwr)

    def sz_send(j, carry):
        zz = near(far_offset(j))
        send("sz", 0, szs.at[zz], szr.at[z], at_z(zz))
        return carry

    lax.fori_loop(0, NZ - 1, sz_send, 0)
    szr[z] = szs[z]

    sum_bf = summed.astype(BF)
    sbp[...] = jnp.zeros_like(sbp)
    sbp[pl.ds(0, PER), :] = sum_bf
    dsend[...] = (
        lax.dot_general(hot, sbp[...], (((1,), (1,)), ((), ())), preferred_element_type=F32)
        .astype(BF)
        .reshape(NZ, 16, 128)
    )
    sent("sy", syr.at[pl.ds(0, NY - 1)])
    sent("gy", yr)
    sent("gz", zs)

    w_wait("qw", qwr)
    z_stage("qz", jnp.sum(qwr[...], axis=0), qzs, qzr)

    def d_send(j, carry):
        zz = near(far_offset(j))
        send("dz", 0, dsend.at[zz], dr.at[z], at_z(zz))
        return carry

    lax.fori_loop(0, NZ - 1, d_send, 0)
    dr[z] = dsend[z]

    z_wait("sz", szr)
    low = lax.broadcasted_iota(jnp.int32, (16, 128), 1) < 64
    parts = [[], [], []]
    for pair in range(NZ // 2):
        even0, even1 = szr[2 * pair, pl.ds(0, 16), :].astype(F32), szr[2 * pair, pl.ds(16, 16), :].astype(F32)
        odd0, odd1 = szr[2 * pair + 1, pl.ds(0, 16), :].astype(F32), szr[2 * pair + 1, pl.ds(16, 16), :].astype(F32)
        parts[0].append(jnp.where(low, even0, pltpu.roll(odd0, 64, 1)))
        parts[1].append(jnp.where(low, pltpu.roll(even0, 64, 1), odd0))
        parts[2].append(jnp.where(low, even1, pltpu.roll(odd1, 64, 1)))
    packed = jnp.concatenate([jnp.concatenate(p, axis=1) for p in parts], axis=0).astype(BF)
    target = own_z * 64 + own_y * 16 + slot
    rows = lax.broadcasted_iota(jnp.int32, (NZ * 64, NT), 0)
    old = []
    for a in range(3):
        pick = jnp.where(rows == target + 4 * a, 1.0, 0.0).astype(BF)
        old.append(jnp.dot(packed, pick, preferred_element_type=F32))
    sent("qw", qwr.at[pl.ds(0, NW - 1)])
    sent("sz", szs.at[pl.ds(0, NZ - 1)])

    z_wait("qz", qzr)
    all_squares = jnp.sum(jnp.sum(qzr[...], axis=0), axis=(0, 1), keepdims=True)
    entries = float(NT * R * COLS * NX * NC)
    factor = jnp.minimum(
        1.0, CLIP_RMS * jnp.sqrt(jnp.full((1, 1), entries, F32)) / jnp.sqrt(all_squares + 1e-06)
    )
    step = jnp.full((1, 1), stepv[0].astype(F32), F32)

    new_w, _, _ = adam(sum_bf.astype(F32) * factor, step, old[0], old[1], old[2])
    new_w = new_w.astype(BF)
    wown[...] = new_w
    zg[z] = new_w

    for d in SPREAD:
        send("az", d % NZ, wown, zg.at[z], at_z(near(d)))
    for k in (2, 1, 3):
        send("ay", 0, wown, slice_at(agb, y, z), at_y((y + k) & (NY - 1)))
    peak = jnp.max(jnp.abs(new_w.astype(F32)).reshape(PER // 8, 8, 128), axis=0)
    w_stage("mw", peak, mws, mwr)

    def take(d):
        arrived("az", d % NZ, zg.at[near(-d)])

    def pass_z(d):
        side = 1 if d > 0 else -1
        for s in (3, 2, 1):
            send("az", (d + side * s) % NZ, zg.at[near(-d)], zg.at[near(-d)], at_z(near(side * s)))

    def pass_y(d):
        zz = near(-d)
        for k in (2, 1, 3):
            send("ay", 0, zg.at[zz], slice_at(agb, y, zz), at_y((y + k) & (NY - 1)))

    for d in (1, -1, 2, -2):
        take(d)
        pass_y(d)
    for d in (4, -4):
        take(d)
        pass_z(d)
    for d in (3, -3):
        take(d)
        pass_y(d)
    for d in (4, -4):
        pass_y(d)

    z_wait("dz", dr)
    lane = lax.broadcasted_iota(jnp.int32, (16, 128), 1)
    for b in range(YB):
        block = jnp.zeros((16, 128), F32)
        for zz in range(NZ):
            start = zz * PER - b * 128
            if -PER < start < 128:
                piece = dr[zz].astype(F32)
                if start % 128:
                    piece = pltpu.roll(piece, start % 128, 1)
                if start < 0:
                    piece = jnp.where(lane < start + PER, piece, 0.0)
                elif start + PER > 128:
                    piece = jnp.where(lane >= start, piece, 0.0)
                block = block + piece
        dys[:, pl.ds(b * 4, 4), :] = block.reshape(NY, SLOTS, 128)
    for k in (2, 1, 3):
        yy = (y + k) & (NY - 1)
        send("dy", 0, dys.at[yy], dyr.at[y], at_y(yy))
    dyr[y] = dys[y]

    w_wait("mw", mwr)
    z_stage("mz", jnp.max(mwr[...], axis=0), mzs, mzr)
    for d in (5, -5, 8, 6, -6, 7, -7):
        take(d)
        pass_y(d)
    keep_group = pltpu.make_async_copy(
        zg.reshape(YE, NT), agb.at[pl.ds(pl.multiple_of(y * YE, 16), YE)], lsem.at[4 * CB + 2]
    )
    keep_group.start()
    sent("qz", qzr.at[pl.ds(0, NZ - 1)])
    sent("dz", dsend.at[pl.ds(0, NZ - 1)])
    sent("az", zg.at[pl.ds(0, NZ - 1)])
    sent("mw", mwr.at[pl.ds(0, NW - 1)])

    arrived("dy", 0, dyr.at[pl.ds(0, NY - 1)])
    flat = dyr.reshape(NY * YB * SLOTS, 128)
    for s in range(SLOTS):
        rows_s = flat[pl.ds(s, BLKS, stride=SLOTS), :]
        s2[:, pl.ds(s * R, R), :] = rows_s.reshape(CB, R, 128)
    sums = s2[...].reshape(CB * SLOTS * R, 128)
    size = CB * SLOTS * R
    olds = [sf[pl.ds(a * size, size), :] for a in range(3)]
    news = adam(sums * factor, step, *olds)
    slot_row = (lax.broadcasted_iota(jnp.int32, (size, 128), 0) // R) % SLOTS
    live = slot_row.astype(F32) < count
    nvs2 = nvs.reshape(3, size, 128)
    for a in range(3):
        nvs2[a] = jnp.where(live, news[a], olds[a]).astype(BF)
    keep_new = pltpu.make_async_copy(nvs, nv, lsem.at[4 * CB])
    keep_new.start()

    z_wait("mz", mzr)
    peakv[...] = jnp.max(jnp.max(mzr[...], axis=0), axis=0, keepdims=True) + PEAK_EPS
    keep_peak = pltpu.make_async_copy(peakv, peak_ref, lsem.at[4 * CB + 1])
    keep_peak.start()
    sent("dy", dys.at[pl.ds(0, NY - 1)])
    sent("mz", mzr.at[pl.ds(0, NZ - 1)])
    keep_new.wait()
    keep_peak.wait()
    keep_group.wait()
    arrived("ay", 0, agb.at[pl.ds(0, (NY - 1) * NZ * PER)])
    sent("ay", agb.at[pl.ds(0, (NY - 1) * NZ * PER)])


def finish(agb, nv, peak_ref, nw_ref, nm_ref, nv_ref, quant_ref, scale_ref, peakv, nvv, tv, fs, ov, sem):
    outs = (nw_ref, nm_ref, nv_ref)

    def o_copy(a, cb):
        return pltpu.make_async_copy(
            nvv.at[a, cb], outs[a].at[:, :, pl.ds(cb * 128, 128)], sem.at[CB + a * CB + cb]
        )

    def t_copy(cb):
        rows = pl.ds(cb * R * 128, R * 128)
        return pltpu.make_async_copy(agb.at[rows], tv.at[rows], sem.at[cb])

    def q_copy(cb):
        return pltpu.make_async_copy(ov.at[cb], quant_ref.at[:, :, pl.ds(cb * 128, 128)], sem.at[cb])

    peak_copy = pltpu.make_async_copy(peak_ref, peakv, sem.at[4 * CB])
    peak_copy.start()
    nv_copy = pltpu.make_async_copy(nv, nvv, sem.at[4 * CB + 1])
    for cb in range(CB):
        t_copy(cb).start()
    nv_copy.start()
    peak_copy.wait()
    keep_peak = pltpu.make_async_copy(peakv, scale_ref, sem.at[4 * CB])
    keep_peak.start()
    nv_copy.wait()
    for a in range(3):
        for cb in range(CB):
            o_copy(a, cb).start()
    inverse = 1.0 / peakv[...]
    o2 = ov.reshape(CB, NT * R, 128)
    for cb in range(CB):
        t_copy(cb).wait()
        for r in range(R):
            block = tv[pl.ds((cb * R + r) * 128, 128), :].astype(F32) * inverse
            fs[pl.ds(r, NT, stride=R), :] = block.T
        o2[cb] = fs[...].astype(BF)
        q_copy(cb).start()
    for a in range(3):
        for cb in range(CB):
            o_copy(a, cb).wait()
    for cb in range(CB):
        q_copy(cb).wait()
    keep_peak.wait()


def local(grad_values, grad_scales, owner_ids, step_count, master, moment1, moment2):
    hbm = pl.BlockSpec(memory_space=pltpu.HBM)
    owned = jax.ShapeDtypeStruct((SLOTS, R, COLS), BF)
    V = pltpu.VMEM
    one = V((8, 128), F32)
    exchange = [one, V((NW, 8, 128), F32), one, V((NZ, 8, 128), F32)]
    agb, news, peaks = pl.pallas_call(
        kernel,
        out_shape=(
            jax.ShapeDtypeStruct((E, NT), BF),
            jax.ShapeDtypeStruct((3, CB, SLOTS, R, 128), BF),
            jax.ShapeDtypeStruct((1, NT), F32),
        ),
        in_specs=[hbm] * 7,
        out_specs=(hbm, hbm, hbm),
        scratch_shapes=[
            V((CB, NT, R, 128), BF),
            V((1, NT), F32),
            V((1, NT), jnp.int32),
            pltpu.SMEM((1,), jnp.int32),
            V((1, NT), F32),
            V((NT * R, 128), F32),
            V((E, NT), BF),
            V((3, CB, SLOTS, R, 128), BF),
            V((3 * CB * SLOTS * R, 128), F32),
            V((CB, R * 16, 128), F32),
            V((NY, YB * 16, 128), BF),
            V((NY, YB * 16, 128), BF),
            V((YE, 128), F32),
            V((NZ, 32, 128), BF),
            V((NZ, 32, 128), BF),
            V((NZ, 3, PER, NT), BF),
            V((NZ - 1, PER, NT), BF),
            V((2, 4, PER, NT), BF),
            V((len(DIRECT) - 1, PER, NT), BF),
            V((128, NT), BF),
            V((NZ, 16, 128), BF),
            V((NZ, 16, 128), BF),
            V((NY, YB * SLOTS, 128), F32),
            V((NY, YB * SLOTS, 128), F32),
            V((CB, SLOTS * R, 128), F32),
            V((3, CB, SLOTS, R, 128), BF),
        ]
        + exchange
        + exchange
        + [
            V((PER, NT), BF),
            V((NZ, PER, NT), BF),
            pltpu.SemaphoreType.DMA((4 * CB + 3,)),
            pltpu.SemaphoreType.DMA((len(KINDS),)),
            pltpu.SemaphoreType.DMA((_total,)),
            pltpu.SemaphoreType.REGULAR,
        ],
        compiler_params=pltpu.CompilerParams(
            collective_id=0, has_side_effects=True, vmem_limit_bytes=62 << 20
        ),
        name="exchange",
    )(
        grad_values[0], grad_scales, owner_ids.reshape(1, NT), step_count,
        master[0], moment1[0], moment2[0],
    )
    out = pl.pallas_call(
        finish,
        out_shape=(
            owned, owned, owned,
            jax.ShapeDtypeStruct((NT, R, COLS), BF),
            jax.ShapeDtypeStruct((1, NT), F32),
        ),
        in_specs=[hbm, hbm, hbm],
        out_specs=(hbm,) * 5,
        scratch_shapes=[
            V((1, NT), F32),
            V((3, CB, SLOTS, R, 128), BF),
            V((E, NT), BF),
            V((NT * R, 128), F32),
            V((CB, NT, R, 128), BF),
            pltpu.SemaphoreType.DMA((4 * CB + 2,)),
        ],
        compiler_params=pltpu.CompilerParams(vmem_limit_bytes=62 << 20),
        name="finish",
    )(agb, news, peaks)
    return out[0][None], out[1][None], out[2][None], out[3], out[4].reshape(NT)


def solution(mesh):
    split = P("dp", None, None, "tensor")
    return jax.shard_map(
        local,
        mesh=mesh,
        in_specs=(split, P("dp", None), P(), P(), split, split, split),
        out_specs=(split, split, split, P(None, None, "tensor"), P()),
        check_vma=False,
    )
```

```python
import jax
import jax.numpy as jnp
from jax import lax
from jax.experimental import pallas as pl
from jax.experimental.pallas import tpu as pltpu
from jax.sharding import PartitionSpec as P

BETA_ONE = 0.9
BETA_TWO = 0.95
RATE = 0.1
DECAY = 0.1
ADAM_EPS = 1e-08
PEAK_EPS = 1e-06
CLIP_RMS = 0.5

NY, NZ, NX, NC = 4, 16, 4, 2
NT, SLOTS, R, COLS = 128, 4, 4, 768
CB = COLS // 128
BLKS = CB * R
E = BLKS * 128
YE = E // NY
PER = YE // NZ
YB = BLKS // NY
MESH = pl.DeviceIdType.MESH
BF, F32 = jnp.bfloat16, jnp.float32

KINDS = ("sy", "sz", "gn", "gy", "gz", "qw", "qz", "dz", "dy", "az", "ay", "mw", "mz")
SEND = {name: i for i, name in enumerate(KINDS)}
RECV, _total = {}, 0
for _name in KINDS:
    if _name == "az":
        RECV[_name] = RECV["gy"]
        continue
    RECV[_name] = _total
    _total += {"gy": NZ, "gz": 3}.get(_name, 1)
NW = NY * NX * NC
CLOSE = (2, -2, 1, -1)
DIRECT = (8, 4, -4, 3, -3, 0)
SPREAD = (4, -4, 1, -1, 8, 2, -2, 3, -3)


def far_offset(j):
    return 8 + (1 - 2 * (j & 1)) * ((j + 1) >> 1)


def relayed(i):
    return 1 - 2 * (i & 1), 7 - (i >> 1)


def adam(g, step, master, first, second):
    m = BETA_ONE * first + (1.0 - BETA_ONE) * g
    v = BETA_TWO * second + (1.0 - BETA_TWO) * g * g
    one = 1.0 - jnp.exp(step * jnp.log(jnp.full_like(step, BETA_ONE)))
    two = 1.0 - jnp.exp(step * jnp.log(jnp.full_like(step, BETA_TWO)))
    m_hat = m / one
    v_hat = v / two
    w = master - RATE * (m_hat / (jnp.sqrt(v_hat) + ADAM_EPS) + DECAY * master)
    return w, m, v


def kernel(
    g_ref, gs_ref, own_ref, step_ref, w_ref, m_ref, v_ref,
    agb, nv, peak_ref,
    gv, gsv, ownv, stepv, peakv, fs, tv, sv, sf, ysf, ys, syr, st, szs, szr,
    nb, close, closeb, yr, zs, rr, zr, sbp, dsend, dr, dys, dyr, s2, nvs,
    qws, qwr, qzs, qzr, mws, mwr, mzs, mzr,
    wown, zg,
    lsem, ssem, rsem, ready,
):
    dp, tp = lax.axis_index("dp"), lax.axis_index("tensor")
    y, z = dp >> 4, dp & (NZ - 1)
    w_me = y * (NX * NC) + tp

    def at_z(zz):
        return (y * NZ + zz, tp)

    def at_y(yy):
        return (yy * NZ + z, tp)

    def at_w(k):
        return (((y + (k >> 3)) & (NY - 1)) * NZ + z, (tp + k) & (NX * NC - 1))

    def near(d):
        return (z + d + NZ) & (NZ - 1)

    def send(kind, i, src, dst, dev):
        pltpu.make_async_remote_copy(
            src_ref=src, dst_ref=dst, send_sem=ssem.at[SEND[kind]],
            recv_sem=rsem.at[RECV[kind] + i], device_id=dev, device_id_type=MESH,
        ).start()

    def arrived(kind, i, ref):
        pltpu.make_async_copy(ref, ref, rsem.at[RECV[kind] + i]).wait()

    def sent(kind, ref):
        pltpu.make_async_copy(ref, ref, ssem.at[SEND[kind]]).wait()

    barrier = pltpu.get_barrier_semaphore()

    def greet(device):
        pl.semaphore_signal(barrier, inc=1, device_id=device, device_id_type=MESH)

    for d in (4, -4, 3, -3, 2, -2, 1, -1):
        greet(at_z(near(d)))
    for k in (4, 5, 3, 2, 6, 7, 1):
        greet(at_w(k))
    for k in (2, 1, 3):
        greet(at_y((y + k) & (NY - 1)))

    state = (w_ref, m_ref, v_ref)

    def g_copy(cb):
        return pltpu.make_async_copy(g_ref.at[:, :, pl.ds(cb * 128, 128)], gv.at[cb], lsem.at[cb])

    def s_copy(a, cb):
        return pltpu.make_async_copy(
            state[a].at[:, :, pl.ds(cb * 128, 128)], sv.at[a, cb], lsem.at[CB]
        )

    gs_copy = pltpu.make_async_copy(gs_ref, gsv, lsem.at[CB + 1])
    own_copy = pltpu.make_async_copy(own_ref, ownv, lsem.at[CB + 2])
    gs_copy.start()
    for cb in range(CB):
        g_copy(cb).start()
    own_copy.start()
    step_copy = pltpu.make_async_copy(step_ref, stepv, lsem.at[CB + 3])
    step_copy.start()
    for a in range(3):
        for cb in range(CB):
            s_copy(a, cb).start()

    gs_copy.wait()
    scales = jnp.broadcast_to(gsv[...], (NT, NT)).T
    g2 = gv.reshape(CB, NT * R, 128)
    for cb in range(CB):
        g_copy(cb).wait()
        fs[...] = g2[cb].astype(F32)
        for r in range(R):
            block = fs[pl.ds(r, NT, stride=R), :]
            tv[pl.ds((cb * R + r) * 128, 128), :] = (block * scales).astype(BF).T

    pltpu.make_async_copy(sv, sv, lsem.at[CB]).wait()
    sf[...] = sv.reshape(3 * CB * SLOTS * R, 128)[...].astype(F32)
    ysf[...] = jnp.zeros_like(ysf)
    for a in range(3):
        for r in range(R):
            rows = sf[pl.ds(a * CB * SLOTS * R + r, CB * SLOTS, stride=R), :]
            ysf[:, pl.ds(r * 16 + a * 4, 4), :] = rows.reshape(CB, SLOTS, 128)
    ys[...] = ysf[...].reshape(NY, YB * 16, 128).astype(BF)

    pl.semaphore_wait(barrier, 8 + (NX * NC - 1) + (NY - 1))

    for k in range(1, NY):
        yy = (y + k) & (NY - 1)
        send("sy", 0, ys.at[yy], syr.at[y], at_y(yy))
    syr[y] = ys[y]

    tv4 = tv.reshape(NY, NZ, PER, NT)
    for i, d in enumerate(CLOSE):
        send("gn", 0, tv4.at[:, near(d)], nb.at[i], at_z(near(d)))

    def slice_at(ref, yy, zz):
        return ref.at[pl.ds(pl.multiple_of((yy * NZ + zz) * PER, 16), PER)]

    def y_send(i, zz):
        for k in (2, 1, 3):
            yy = (y + k) & (NY - 1)
            send("gy", i, slice_at(tv, yy, zz), yr.at[i, k - 1], at_y(yy))

    def y_send_relayed(i, carry):
        side, far = relayed(i)
        y_send(i, near(side * far))
        return carry

    lax.fori_loop(0, 6, y_send_relayed, 0)
    for i, d in enumerate(DIRECT[:-1]):
        y_send(6 + i, near(d))

    for d in (4, -4):
        pl.semaphore_signal(ready, inc=1, device_id=at_z(near(d)), device_id_type=MESH)

    def y_sum(i, total):
        arrived("gy", i, yr.at[i])
        for k in range(3):
            total = total + yr[i, k].astype(F32)
        return total

    def part_of(zz):
        return slice_at(tv, y, zz)[...].astype(F32)

    def to_relay(i, carry):
        side, far = relayed(i)
        zs[i] = y_sum(i, part_of(near(side * far))).astype(BF)
        send("gz", 1 + (i & 1), zs.at[i], rr.at[i & 1, i >> 1], at_z(near(side * (far - 4))))
        return carry

    lax.fori_loop(0, 2, to_relay, 0)

    arrived("gn", 0, nb)
    for yy in range(NY):
        total = tv4[yy, z].astype(F32)
        for i in range(len(CLOSE)):
            total = total + nb[i, yy].astype(F32)
        close[yy] = total
        closeb[yy] = total.astype(BF)
    last = 6 + len(DIRECT) - 1
    for k in (2, 1, 3):
        yy = (y + k) & (NY - 1)
        send("gy", last, closeb.at[yy], yr.at[last, k - 1], at_y(yy))

    lax.fori_loop(2, 6, to_relay, 0)
    pl.semaphore_wait(ready, 2)
    for i, d in enumerate(DIRECT[:-1]):
        total = y_sum(6 + i, part_of(near(d)))
        if abs(d) == 4:
            side = 0 if d > 0 else 1
            arrived("gz", 1 + side, rr.at[side])
            for k in range(3):
                total = total + rr[side, k].astype(F32)
        zs[6 + i] = total.astype(BF)
        send("gz", 0, zs.at[6 + i], zr.at[i], at_z(near(d)))
    mine = y_sum(last, close[y])

    arrived("sy", 0, syr.at[pl.ds(0, NY - 1)])
    for b in range(YB):
        block = syr[:, pl.ds(b * 16, 16), :].reshape(NY * 16, 128).astype(F32)
        block = jnp.concatenate([block, jnp.zeros((128 - NY * 16, 128), F32)], axis=0)
        st[pl.ds(b * 128, 128), :] = block.T
    for zz in range(NZ):
        upper = st[pl.ds(zz * PER, 16), :] + pltpu.roll(st[pl.ds(zz * PER + 16, 16), :], 64, 1)
        szs[zz, pl.ds(0, 16), :] = upper.astype(BF)
        szs[zz, pl.ds(16, 16), :] = st[pl.ds(zz * PER + 32, 16), :].astype(BF)

    own_copy.wait()
    step_copy.wait()
    own = ownv[...]
    spread = jnp.broadcast_to(own.astype(F32), (NT, NT))
    same = spread == spread.T
    before = lax.broadcasted_iota(jnp.int32, (NT, NT), 0) < lax.broadcasted_iota(jnp.int32, (NT, NT), 1)
    slot = jnp.sum(jnp.where(same & before, 1.0, 0.0), axis=0, keepdims=True).astype(jnp.int32)
    own_z, own_y = own & (NZ - 1), own >> 4
    count = jnp.sum(jnp.where(own == dp, 1.0, 0.0), axis=1, keepdims=True)
    place = own_z * 16 + own_y * 4 + slot
    hot = jnp.where(
        lax.broadcasted_iota(jnp.int32, (NZ * 16, NT), 0) == place, 1.0, 0.0
    ).astype(BF)

    arrived("gz", 0, zr)
    summed = mine
    for i in range(len(DIRECT) - 1):
        summed = summed + zr[i].astype(F32)

    def w_stage(kind, value, sendbuf, buf):
        sendbuf[...] = value
        buf[w_me] = value

        def body(i, carry):
            send(kind, 0, sendbuf, buf.at[w_me], at_w(NW - 1 - i))
            return carry

        lax.fori_loop(0, NW - 1, body, 0)

    def w_wait(kind, buf):
        arrived(kind, 0, buf.at[pl.ds(0, NW - 1)])

    def z_stage(kind, value, sendbuf, buf):
        sendbuf[...] = value
        buf[z] = value

        def body(j, carry):
            send(kind, 0, sendbuf, buf.at[z], at_z(near(far_offset(j))))
            return carry

        lax.fori_loop(0, NZ - 1, body, 0)

    def z_wait(kind, buf):
        arrived(kind, 0, buf.at[pl.ds(0, NZ - 1)])

    squares = jnp.sum(summed * summed, axis=0, keepdims=True)
    w_stage("qw", squares, qws, qwr)

    def sz_send(j, carry):
        zz = near(far_offset(j))
        send("sz", 0, szs.at[zz], szr.at[z], at_z(zz))
        return carry

    lax.fori_loop(0, NZ - 1, sz_send, 0)
    szr[z] = szs[z]

    sum_bf = summed.astype(BF)
    sbp[...] = jnp.zeros_like(sbp)
    sbp[pl.ds(0, PER), :] = sum_bf
    dsend[...] = (
        lax.dot_general(hot, sbp[...], (((1,), (1,)), ((), ())), preferred_element_type=F32)
        .astype(BF)
        .reshape(NZ, 16, 128)
    )
    sent("sy", syr.at[pl.ds(0, NY - 1)])
    sent("gn", nb)
    sent("gy", yr)
    sent("gz", zs)

    w_wait("qw", qwr)
    z_stage("qz", jnp.sum(qwr[...], axis=0), qzs, qzr)

    def d_send(j, carry):
        zz = near(far_offset(j))
        send("dz", 0, dsend.at[zz], dr.at[z], at_z(zz))
        return carry

    lax.fori_loop(0, NZ - 1, d_send, 0)
    dr[z] = dsend[z]

    z_wait("sz", szr)
    low = lax.broadcasted_iota(jnp.int32, (16, 128), 1) < 64
    parts = [[], [], []]
    for pair in range(NZ // 2):
        even0, even1 = szr[2 * pair, pl.ds(0, 16), :].astype(F32), szr[2 * pair, pl.ds(16, 16), :].astype(F32)
        odd0, odd1 = szr[2 * pair + 1, pl.ds(0, 16), :].astype(F32), szr[2 * pair + 1, pl.ds(16, 16), :].astype(F32)
        parts[0].append(jnp.where(low, even0, pltpu.roll(odd0, 64, 1)))
        parts[1].append(jnp.where(low, pltpu.roll(even0, 64, 1), odd0))
        parts[2].append(jnp.where(low, even1, pltpu.roll(odd1, 64, 1)))
    packed = jnp.concatenate([jnp.concatenate(p, axis=1) for p in parts], axis=0).astype(BF)
    target = own_z * 64 + own_y * 16 + slot
    rows = lax.broadcasted_iota(jnp.int32, (NZ * 64, NT), 0)
    old = []
    for a in range(3):
        pick = jnp.where(rows == target + 4 * a, 1.0, 0.0).astype(BF)
        old.append(jnp.dot(packed, pick, preferred_element_type=F32))
    sent("qw", qwr.at[pl.ds(0, NW - 1)])
    sent("sz", szs.at[pl.ds(0, NZ - 1)])

    z_wait("qz", qzr)
    all_squares = jnp.sum(jnp.sum(qzr[...], axis=0), axis=(0, 1), keepdims=True)
    entries = float(NT * R * COLS * NX * NC)
    factor = jnp.minimum(
        1.0, CLIP_RMS * jnp.sqrt(jnp.full((1, 1), entries, F32)) / jnp.sqrt(all_squares + 1e-06)
    )
    step = stepv[...].astype(F32)

    new_w, _, _ = adam(sum_bf.astype(F32) * factor, step, old[0], old[1], old[2])
    new_w = new_w.astype(BF)
    wown[...] = new_w
    zg[z] = new_w

    for d in SPREAD:
        send("az", d % NZ, wown, zg.at[z], at_z(near(d)))
    peak = jnp.max(jnp.abs(new_w.astype(F32)), axis=0, keepdims=True)
    w_stage("mw", peak, mws, mwr)
    for k in (2, 1, 3):
        send("ay", 0, wown, slice_at(agb, y, z), at_y((y + k) & (NY - 1)))

    def take(d):
        arrived("az", d % NZ, zg.at[near(-d)])

    def pass_z(d):
        side = 1 if d > 0 else -1
        for s in (3, 2, 1):
            send("az", (d + side * s) % NZ, zg.at[near(-d)], zg.at[near(-d)], at_z(near(side * s)))

    def pass_y(d):
        zz = near(-d)
        for k in (2, 1, 3):
            send("ay", 0, zg.at[zz], slice_at(agb, y, zz), at_y((y + k) & (NY - 1)))

    for d in (1, -1, 2, -2):
        take(d)
        pass_y(d)
    for d in (4, -4):
        take(d)
        pass_z(d)
    for d in (3, -3):
        take(d)
        pass_y(d)
    for d in (4, -4):
        pass_y(d)

    z_wait("dz", dr)
    lane = lax.broadcasted_iota(jnp.int32, (16, 128), 1)
    for b in range(YB):
        block = jnp.zeros((16, 128), F32)
        for zz in range(NZ):
            start = zz * PER - b * 128
            if -PER < start < 128:
                piece = dr[zz].astype(F32)
                if start % 128:
                    piece = pltpu.roll(piece, start % 128, 1)
                if start < 0:
                    piece = jnp.where(lane < start + PER, piece, 0.0)
                elif start + PER > 128:
                    piece = jnp.where(lane >= start, piece, 0.0)
                block = block + piece
        dys[:, pl.ds(b * 4, 4), :] = block.reshape(NY, SLOTS, 128)
    for k in (2, 1, 3):
        yy = (y + k) & (NY - 1)
        send("dy", 0, dys.at[yy], dyr.at[y], at_y(yy))
    dyr[y] = dys[y]

    w_wait("mw", mwr)
    z_stage("mz", jnp.max(mwr[...], axis=0), mzs, mzr)
    for d in (5, -5, 8, 6, -6, 7, -7):
        take(d)
        pass_y(d)
    keep_group = pltpu.make_async_copy(
        zg.reshape(YE, NT), agb.at[pl.ds(pl.multiple_of(y * YE, 16), YE)], lsem.at[CB + 3]
    )
    keep_group.start()
    sent("qz", qzr.at[pl.ds(0, NZ - 1)])
    sent("dz", dsend.at[pl.ds(0, NZ - 1)])
    sent("az", zg.at[pl.ds(0, NZ - 1)])
    sent("mw", mwr.at[pl.ds(0, NW - 1)])

    arrived("dy", 0, dyr.at[pl.ds(0, NY - 1)])
    flat = dyr.reshape(NY * YB * SLOTS, 128)
    for s in range(SLOTS):
        rows_s = flat[pl.ds(s, BLKS, stride=SLOTS), :]
        s2[:, pl.ds(s * R, R), :] = rows_s.reshape(CB, R, 128)
    sums = s2[...].reshape(CB * SLOTS * R, 128)
    size = CB * SLOTS * R
    olds = [sf[pl.ds(a * size, size), :] for a in range(3)]
    news = adam(sums * factor, step, *olds)
    slot_row = (lax.broadcasted_iota(jnp.int32, (size, 128), 0) // R) % SLOTS
    live = slot_row.astype(F32) < count
    for a in range(3):
        kept = jnp.where(live, news[a], olds[a]).reshape(CB, SLOTS, R, 128).astype(BF)
        for cb in range(CB):
            nvs[a, :, :, pl.ds(cb * 128, 128)] = kept[cb]
    keep_new = pltpu.make_async_copy(nvs, nv, lsem.at[CB + 1])
    keep_new.start()

    z_wait("mz", mzr)
    peakv[...] = jnp.max(mzr[...], axis=0) + PEAK_EPS
    keep_peak = pltpu.make_async_copy(peakv, peak_ref, lsem.at[CB + 2])
    keep_peak.start()
    sent("dy", dys.at[pl.ds(0, NY - 1)])
    sent("mz", mzr.at[pl.ds(0, NZ - 1)])
    keep_new.wait()
    keep_peak.wait()
    keep_group.wait()
    arrived("ay", 0, agb.at[pl.ds(0, (NY - 1) * NZ * PER)])
    sent("ay", agb.at[pl.ds(0, (NY - 1) * NZ * PER)])


def finish(
    agb, nv, peak_ref, nw_ref, nm_ref, nv_ref, quant_ref, scale_ref, peakv, nvv, tv, fs, ov, sem
):
    outs = (nw_ref, nm_ref, nv_ref)

    def o_copy(a):
        return pltpu.make_async_copy(nvv.at[a], outs[a], sem.at[CB])

    def t_copy(cb):
        rows = pl.ds(cb * R * 128, R * 128)
        return pltpu.make_async_copy(agb.at[rows], tv.at[rows], sem.at[cb])

    def q_copy(cb):
        return pltpu.make_async_copy(
            ov.at[cb], quant_ref.at[:, :, pl.ds(cb * 128, 128)], sem.at[CB + 1]
        )

    peak_copy = pltpu.make_async_copy(peak_ref, peakv, sem.at[CB + 2])
    peak_copy.start()
    for cb in range(CB):
        t_copy(cb).start()
    nv_copy = pltpu.make_async_copy(nv, nvv, sem.at[CB])
    nv_copy.start()
    peak_copy.wait()
    keep_peak = pltpu.make_async_copy(peakv, scale_ref, sem.at[CB + 2])
    keep_peak.start()
    inverse = jnp.broadcast_to(1.0 / peakv[...], (NT, NT)).T
    o2 = ov.reshape(CB, NT * R, 128)
    for cb in range(CB):
        t_copy(cb).wait()
        for r in range(R):
            block = tv[pl.ds((cb * R + r) * 128, 128), :].T
            fs[pl.ds(r, NT, stride=R), :] = block.astype(F32) * inverse
        o2[cb] = fs[...].astype(BF)
        q_copy(cb).start()
        if cb == 0:
            nv_copy.wait()
            for a in range(3):
                o_copy(a).start()
    keep_peak.wait()
    pltpu.make_async_copy(nvv, nvv, sem.at[CB]).wait()
    pltpu.make_async_copy(ov, ov, sem.at[CB + 1]).wait()


def local(grad_values, grad_scales, owner_ids, step_count, master, moment1, moment2):
    hbm = pl.BlockSpec(memory_space=pltpu.HBM)
    owned = jax.ShapeDtypeStruct((SLOTS, R, COLS), BF)
    V = pltpu.VMEM
    one = V((1, 128), F32)
    exchange = [one, V((NW, 1, 128), F32), one, V((NZ, 1, 128), F32)]
    agb, news, peaks = pl.pallas_call(
        kernel,
        out_shape=(
            jax.ShapeDtypeStruct((E, NT), BF),
            jax.ShapeDtypeStruct((3, SLOTS, R, COLS), BF),
            jax.ShapeDtypeStruct((1, NT), F32),
        ),
        in_specs=[hbm] * 7,
        out_specs=(hbm, hbm, hbm),
        scratch_shapes=[
            V((CB, NT, R, 128), BF),
            V((1, NT), F32),
            V((1, NT), jnp.int32),
            V((1, 1), jnp.int32),
            V((1, NT), F32),
            V((NT * R, 128), F32),
            V((E, NT), BF),
            V((3, CB, SLOTS, R, 128), BF),
            V((3 * CB * SLOTS * R, 128), F32),
            V((CB, R * 16, 128), F32),
            V((NY, YB * 16, 128), BF),
            V((NY, YB * 16, 128), BF),
            V((YE, 128), F32),
            V((NZ, 32, 128), BF),
            V((NZ, 32, 128), BF),
            V((len(CLOSE), NY, PER, NT), BF),
            V((NY, PER, NT), F32),
            V((NY, PER, NT), BF),
            V((6 + len(DIRECT), 3, PER, NT), BF),
            V((5 + len(DIRECT), PER, NT), BF),
            V((2, 3, PER, NT), BF),
            V((len(DIRECT) - 1, PER, NT), BF),
            V((128, NT), BF),
            V((NZ, 16, 128), BF),
            V((NZ, 16, 128), BF),
            V((NY, YB * SLOTS, 128), F32),
            V((NY, YB * SLOTS, 128), F32),
            V((CB, SLOTS * R, 128), F32),
            V((3, SLOTS, R, COLS), BF),
        ]
        + exchange
        + exchange
        + [
            V((PER, NT), BF),
            V((NZ, PER, NT), BF),
            pltpu.SemaphoreType.DMA((CB + 4,)),
            pltpu.SemaphoreType.DMA((len(KINDS),)),
            pltpu.SemaphoreType.DMA((_total,)),
            pltpu.SemaphoreType.REGULAR,
        ],
        compiler_params=pltpu.CompilerParams(
            collective_id=0, has_side_effects=True, vmem_limit_bytes=62 << 20
        ),
        name="exchange",
    )(
        grad_values[0], grad_scales, owner_ids.reshape(1, NT), step_count.reshape(1, 1),
        master[0], moment1[0], moment2[0],
    )
    out = pl.pallas_call(
        finish,
        out_shape=(
            owned, owned, owned,
            jax.ShapeDtypeStruct((NT, R, COLS), BF),
            jax.ShapeDtypeStruct((1, NT), F32),
        ),
        in_specs=[hbm, hbm, hbm],
        out_specs=(hbm,) * 5,
        scratch_shapes=[
            V((1, NT), F32),
            V((3, SLOTS, R, COLS), BF),
            V((E, NT), BF),
            V((NT * R, 128), F32),
            V((CB, NT, R, 128), BF),
            pltpu.SemaphoreType.DMA((CB + 3,)),
        ],
        compiler_params=pltpu.CompilerParams(vmem_limit_bytes=62 << 20),
        name="finish",
    )(agb, news, peaks)
    return out[0][None], out[1][None], out[2][None], out[3], out[4].reshape(NT)


def solution(mesh):
    split = P("dp", None, None, "tensor")
    return jax.shard_map(
        local,
        mesh=mesh,
        in_specs=(split, P("dp", None), P(), P(), split, split, split),
        out_specs=(split, split, split, P(None, None, "tensor"), P()),
        check_vma=False,
    )
```

```python
import jax
import jax.numpy as jnp
from jax import lax
from jax.experimental import pallas as pl
from jax.experimental.pallas import tpu as pltpu
from jax.sharding import PartitionSpec as P

BETA_ONE = 0.9
BETA_TWO = 0.95
RATE = 0.1
DECAY = 0.1
ADAM_EPS = 1e-08
PEAK_EPS = 1e-06
CLIP_RMS = 0.5

NY, NZ, NX, NC = 4, 16, 4, 2
NT, SLOTS, R, COLS = 128, 4, 4, 768
CB = COLS // 128
BLKS = CB * R
E = BLKS * 128
YE = E // NY
PER = YE // NZ
YB = BLKS // NY
MESH = pl.DeviceIdType.MESH
BF, F32 = jnp.bfloat16, jnp.float32

KINDS = ("sy", "sz", "gn", "gy", "gz", "qw", "qz", "dz", "dy", "az", "ay", "an", "ac", "mw", "mz")
SEND = {name: i for i, name in enumerate(KINDS)}
RECV, _total = {}, 0
for _name in KINDS:
    if _name == "az":
        RECV[_name] = RECV["gy"]
        continue
    RECV[_name] = _total
    _total += {"gy": NZ, "gz": 3}.get(_name, 1)
NW = NY * NX * NC
CLOSE = (2, -2, 1, -1)
DIRECT = (8, 3, -3, 4, -4, 0)
WITH_Y = (1, -1)
SPREAD = (4, -4, 8, 2, -2, 3, -3)


def far_offset(j):
    return 8 + (1 - 2 * (j & 1)) * ((j + 1) >> 1)


def relayed(i):
    return 1 - 2 * (i & 1), 7 - (i >> 1)


def adam(g, step, master, first, second):
    m = BETA_ONE * first + (1.0 - BETA_ONE) * g
    v = BETA_TWO * second + (1.0 - BETA_TWO) * g * g
    one = 1.0 - jnp.exp(step * jnp.log(jnp.full_like(step, BETA_ONE)))
    two = 1.0 - jnp.exp(step * jnp.log(jnp.full_like(step, BETA_TWO)))
    m_hat = m / one
    v_hat = v / two
    w = master - RATE * (m_hat / (jnp.sqrt(v_hat) + ADAM_EPS) + DECAY * master)
    return w, m, v


def kernel(
    g_ref, gs_ref, own_ref, step_ref, w_ref, m_ref, v_ref,
    agb, nv, peak_ref,
    gv, gsv, ownv, stepv, peakv, fs, tv, sv, sf, ysf, ys, syr, st, szs, szr,
    nb, close, closeb, yr, zs, rr, zr, sbp, dsend, dr, dys, dyr, s2, nvs,
    qws, qwr, qzs, qzr, mws, mwr, mzs, mzr,
    wown, zg, zn,
    lsem, ssem, rsem, ready, ready_far,
):
    dp, tp = lax.axis_index("dp"), lax.axis_index("tensor")
    y, z = dp >> 4, dp & (NZ - 1)
    w_me = y * (NX * NC) + tp

    def at_z(zz):
        return (y * NZ + zz, tp)

    def at_y(yy):
        return (yy * NZ + z, tp)

    def at_w(k):
        return (((y + (k >> 3)) & (NY - 1)) * NZ + z, (tp + k) & (NX * NC - 1))

    def near(d):
        return (z + d + NZ) & (NZ - 1)

    def send(kind, i, src, dst, dev):
        pltpu.make_async_remote_copy(
            src_ref=src, dst_ref=dst, send_sem=ssem.at[SEND[kind]],
            recv_sem=rsem.at[RECV[kind] + i], device_id=dev, device_id_type=MESH,
        ).start()

    def arrived(kind, i, ref):
        pltpu.make_async_copy(ref, ref, rsem.at[RECV[kind] + i]).wait()

    def sent(kind, ref):
        pltpu.make_async_copy(ref, ref, ssem.at[SEND[kind]]).wait()

    barrier = pltpu.get_barrier_semaphore()

    def greet(device):
        pl.semaphore_signal(barrier, inc=1, device_id=device, device_id_type=MESH)

    for d in (2, -2, 1, -1):
        greet(at_z(near(d)))
    for k in (4, 5, 3, 2, 6, 7, 1):
        greet(at_w(k))
    for k in (2, 1, 3):
        greet(at_y((y + k) & (NY - 1)))

    state = (w_ref, m_ref, v_ref)

    def g_copy(cb):
        return pltpu.make_async_copy(g_ref.at[:, :, pl.ds(cb * 128, 128)], gv.at[cb], lsem.at[cb])

    def s_copy(a, cb):
        return pltpu.make_async_copy(
            state[a].at[:, :, pl.ds(cb * 128, 128)], sv.at[a, cb], lsem.at[CB]
        )

    gs_copy = pltpu.make_async_copy(gs_ref, gsv, lsem.at[CB + 1])
    own_copy = pltpu.make_async_copy(own_ref, ownv, lsem.at[CB + 2])
    gs_copy.start()
    for cb in range(CB):
        g_copy(cb).start()
    own_copy.start()
    step_copy = pltpu.make_async_copy(step_ref, stepv, lsem.at[CB + 3])
    step_copy.start()
    for a in range(3):
        for cb in range(CB):
            s_copy(a, cb).start()

    gs_copy.wait()
    scales = jnp.broadcast_to(gsv[...], (NT, NT)).T
    g2 = gv.reshape(CB, NT * R, 128)
    for cb in range(CB):
        g_copy(cb).wait()
        fs[...] = g2[cb].astype(F32)
        for r in range(R):
            block = fs[pl.ds(r, NT, stride=R), :]
            tv[pl.ds((cb * R + r) * 128, 128), :] = (block * scales).astype(BF).T

    pltpu.make_async_copy(sv, sv, lsem.at[CB]).wait()
    sf[...] = sv.reshape(3 * CB * SLOTS * R, 128)[...].astype(F32)
    ysf[...] = jnp.zeros_like(ysf)
    for a in range(3):
        for r in range(R):
            rows = sf[pl.ds(a * CB * SLOTS * R + r, CB * SLOTS, stride=R), :]
            ysf[:, pl.ds(r * 16 + a * 4, 4), :] = rows.reshape(CB, SLOTS, 128)
    ys[...] = ysf[...].reshape(NY, YB * 16, 128).astype(BF)

    pl.semaphore_wait(barrier, 4 + (NX * NC - 1) + (NY - 1))

    for k in range(1, NY):
        yy = (y + k) & (NY - 1)
        send("sy", 0, ys.at[yy], syr.at[y], at_y(yy))
    syr[y] = ys[y]

    tv4 = tv.reshape(NY, NZ, PER, NT)
    for i, d in enumerate(CLOSE):
        send("gn", 0, tv4.at[:, near(d)], nb.at[i], at_z(near(d)))

    def slice_at(ref, yy, zz):
        return ref.at[pl.ds(pl.multiple_of((yy * NZ + zz) * PER, 16), PER)]

    def y_send(i, zz):
        for k in (1, 3, 2):
            yy = (y + k) & (NY - 1)
            send("gy", i, slice_at(tv, yy, zz), yr.at[i, k - 1], at_y(yy))

    def y_send_relayed(i, carry):
        side, far = relayed(i)
        y_send(i, near(side * far))
        return carry

    lax.fori_loop(0, 6, y_send_relayed, 0)
    for i, d in enumerate(DIRECT[:-1]):
        y_send(6 + i, near(d))

    def tell(sem, hops):
        for d in (hops, -hops):
            pl.semaphore_signal(sem, inc=1, device_id=at_z(near(d)), device_id_type=MESH)

    tell(ready, 2)

    def y_sum(i, total):
        arrived("gy", i, yr.at[i])
        for k in range(3):
            total = total + yr[i, k].astype(F32)
        return total

    def part_of(zz):
        return slice_at(tv, y, zz)[...].astype(F32)

    def to_relay(i, carry):
        side, far = relayed(i)
        zs[i] = y_sum(i, part_of(near(side * far))).astype(BF)
        send("gz", 1 + (i & 1), zs.at[i], rr.at[i & 1, i >> 1], at_z(near(side * (far - 4))))
        return carry

    pl.semaphore_wait(ready, 2)
    tell(ready_far, 4)
    lax.fori_loop(0, 2, to_relay, 0)

    arrived("gn", 0, nb)
    for yy in range(NY):
        total = tv4[yy, z].astype(F32)
        for i in range(len(CLOSE)):
            total = total + nb[i, yy].astype(F32)
        close[yy] = total
        closeb[yy] = total.astype(BF)
    last = 6 + len(DIRECT) - 1
    for k in (2, 1, 3):
        yy = (y + k) & (NY - 1)
        send("gy", last, closeb.at[yy], yr.at[last, k - 1], at_y(yy))

    lax.fori_loop(2, 6, to_relay, 0)
    pl.semaphore_wait(ready_far, 2)
    for i, d in enumerate(DIRECT[:-1]):
        total = y_sum(6 + i, part_of(near(d)))
        if abs(d) == 4:
            side = 0 if d > 0 else 1
            arrived("gz", 1 + side, rr.at[side])
            for k in range(3):
                total = total + rr[side, k].astype(F32)
        zs[6 + i] = total.astype(BF)
        send("gz", 0, zs.at[6 + i], zr.at[i], at_z(near(d)))
    mine = y_sum(last, close[y])

    arrived("sy", 0, syr.at[pl.ds(0, NY - 1)])
    for b in range(YB):
        block = syr[:, pl.ds(b * 16, 16), :].reshape(NY * 16, 128).astype(F32)
        block = jnp.concatenate([block, jnp.zeros((128 - NY * 16, 128), F32)], axis=0)
        st[pl.ds(b * 128, 128), :] = block.T
    for zz in range(NZ):
        upper = st[pl.ds(zz * PER, 16), :] + pltpu.roll(st[pl.ds(zz * PER + 16, 16), :], 64, 1)
        szs[zz, pl.ds(0, 16), :] = upper.astype(BF)
        szs[zz, pl.ds(16, 16), :] = st[pl.ds(zz * PER + 32, 16), :].astype(BF)

    own_copy.wait()
    step_copy.wait()
    own = ownv[...]
    spread = jnp.broadcast_to(own.astype(F32), (NT, NT))
    same = spread == spread.T
    before = lax.broadcasted_iota(jnp.int32, (NT, NT), 0) < lax.broadcasted_iota(jnp.int32, (NT, NT), 1)
    slot = jnp.sum(jnp.where(same & before, 1.0, 0.0), axis=0, keepdims=True).astype(jnp.int32)
    own_z, own_y = own & (NZ - 1), own >> 4
    count = jnp.sum(jnp.where(own == dp, 1.0, 0.0), axis=1, keepdims=True)
    place = own_z * 16 + own_y * 4 + slot
    hot = jnp.where(
        lax.broadcasted_iota(jnp.int32, (NZ * 16, NT), 0) == place, 1.0, 0.0
    ).astype(BF)

    arrived("gz", 0, zr)
    summed = mine
    for i in range(len(DIRECT) - 1):
        summed = summed + zr[i].astype(F32)

    def w_stage(kind, value, sendbuf, buf):
        sendbuf[...] = value
        buf[w_me] = value

        def body(i, carry):
            send(kind, 0, sendbuf, buf.at[w_me], at_w(NW - 1 - i))
            return carry

        lax.fori_loop(0, NW - 1, body, 0)

    def w_wait(kind, buf):
        arrived(kind, 0, buf.at[pl.ds(0, NW - 1)])

    def z_stage(kind, value, sendbuf, buf):
        sendbuf[...] = value
        buf[z] = value

        def body(j, carry):
            send(kind, 0, sendbuf, buf.at[z], at_z(near(far_offset(j))))
            return carry

        lax.fori_loop(0, NZ - 1, body, 0)

    def z_wait(kind, buf):
        arrived(kind, 0, buf.at[pl.ds(0, NZ - 1)])

    squares = jnp.sum(summed * summed, axis=0, keepdims=True)
    w_stage("qw", squares, qws, qwr)

    def sz_send(j, carry):
        zz = near(far_offset(j))
        send("sz", 0, szs.at[zz], szr.at[z], at_z(zz))
        return carry

    lax.fori_loop(0, NZ - 1, sz_send, 0)
    szr[z] = szs[z]

    sum_bf = summed.astype(BF)
    sbp[...] = jnp.zeros_like(sbp)
    sbp[pl.ds(0, PER), :] = sum_bf
    dsend[...] = (
        lax.dot_general(hot, sbp[...], (((1,), (1,)), ((), ())), preferred_element_type=F32)
        .astype(BF)
        .reshape(NZ, 16, 128)
    )
    sent("sy", syr.at[pl.ds(0, NY - 1)])
    sent("gn", nb)
    sent("gy", yr)
    sent("gz", zs)

    w_wait("qw", qwr)
    z_stage("qz", jnp.sum(qwr[...], axis=0), qzs, qzr)

    def d_send(j, carry):
        zz = near(far_offset(j))
        send("dz", 0, dsend.at[zz], dr.at[z], at_z(zz))
        return carry

    lax.fori_loop(0, NZ - 1, d_send, 0)
    dr[z] = dsend[z]

    z_wait("sz", szr)
    low = lax.broadcasted_iota(jnp.int32, (16, 128), 1) < 64
    parts = [[], [], []]
    for pair in range(NZ // 2):
        even0, even1 = szr[2 * pair, pl.ds(0, 16), :].astype(F32), szr[2 * pair, pl.ds(16, 16), :].astype(F32)
        odd0, odd1 = szr[2 * pair + 1, pl.ds(0, 16), :].astype(F32), szr[2 * pair + 1, pl.ds(16, 16), :].astype(F32)
        parts[0].append(jnp.where(low, even0, pltpu.roll(odd0, 64, 1)))
        parts[1].append(jnp.where(low, pltpu.roll(even0, 64, 1), odd0))
        parts[2].append(jnp.where(low, even1, pltpu.roll(odd1, 64, 1)))
    packed = jnp.concatenate([jnp.concatenate(p, axis=1) for p in parts], axis=0).astype(BF)
    target = own_z * 64 + own_y * 16 + slot
    rows = lax.broadcasted_iota(jnp.int32, (NZ * 64, NT), 0)
    old = []
    for a in range(3):
        pick = jnp.where(rows == target + 4 * a, 1.0, 0.0).astype(BF)
        old.append(jnp.dot(packed, pick, preferred_element_type=F32))
    sent("qw", qwr.at[pl.ds(0, NW - 1)])
    sent("sz", szs.at[pl.ds(0, NZ - 1)])

    z_wait("qz", qzr)
    all_squares = jnp.sum(jnp.sum(qzr[...], axis=0), axis=(0, 1), keepdims=True)
    entries = float(NT * R * COLS * NX * NC)
    factor = jnp.minimum(
        1.0, CLIP_RMS * jnp.sqrt(jnp.full((1, 1), entries, F32)) / jnp.sqrt(all_squares + 1e-06)
    )
    step = stepv[...].astype(F32)

    new_w, _, _ = adam(sum_bf.astype(F32) * factor, step, old[0], old[1], old[2])
    new_w = new_w.astype(BF)
    wown[...] = new_w
    zn[y] = new_w

    for d in SPREAD:
        send("az", d % NZ, wown, zg.at[z], at_z(near(d)))
    peak = jnp.max(jnp.abs(new_w.astype(F32)), axis=0, keepdims=True)
    w_stage("mw", peak, mws, mwr)
    for k in (2, 1, 3):
        send("an", 0, wown, zn.at[y], at_y((y + k) & (NY - 1)))

    def take(d):
        zz = near(-d)
        arrived("az", d % NZ, zg.at[zz])
        pltpu.make_async_copy(zg.at[zz], agb.at[y, zz], lsem.at[CB + 3]).start()

    def pass_z(d):
        side = 1 if d > 0 else -1
        for s in (3, 2, 1):
            send("az", (d + side * s) % NZ, zg.at[near(-d)], zg.at[near(-d)], at_z(near(side * s)))

    def pass_y(d):
        zz = near(-d)
        for k in (2, 1, 3):
            send("ay", 0, zg.at[zz], agb.at[y, zz], at_y((y + k) & (NY - 1)))

    arrived("an", 0, zn.at[pl.ds(0, NY - 1)])
    for d in WITH_Y:
        send("ac", 0, zn, agb.at[:, z], at_z(near(d)))
    keep_own = pltpu.make_async_copy(zn, agb.at[:, z], lsem.at[CB + 1])
    keep_own.start()
    for d in (2, -2):
        take(d)
        pass_y(d)
    for d in (4, -4):
        take(d)
        pass_z(d)
    for d in (3, -3):
        take(d)
        pass_y(d)
    for d in (4, -4):
        pass_y(d)

    z_wait("dz", dr)
    lane = lax.broadcasted_iota(jnp.int32, (16, 128), 1)
    for b in range(YB):
        block = jnp.zeros((16, 128), F32)
        for zz in range(NZ):
            start = zz * PER - b * 128
            if -PER < start < 128:
                piece = dr[zz].astype(F32)
                if start % 128:
                    piece = pltpu.roll(piece, start % 128, 1)
                if start < 0:
                    piece = jnp.where(lane < start + PER, piece, 0.0)
                elif start + PER > 128:
                    piece = jnp.where(lane >= start, piece, 0.0)
                block = block + piece
        dys[:, pl.ds(b * 4, 4), :] = block.reshape(NY, SLOTS, 128)
    for k in (2, 1, 3):
        yy = (y + k) & (NY - 1)
        send("dy", 0, dys.at[yy], dyr.at[y], at_y(yy))
    dyr[y] = dys[y]

    w_wait("mw", mwr)
    z_stage("mz", jnp.max(mwr[...], axis=0), mzs, mzr)
    for d in (5, -5, 8, 6, -6, 7, -7):
        take(d)
        pass_y(d)
    sent("qz", qzr.at[pl.ds(0, NZ - 1)])
    sent("dz", dsend.at[pl.ds(0, NZ - 1)])
    keep_own.wait()
    sent("an", zg.at[pl.ds(0, NY - 1)])
    sent("ac", tv.at[pl.ds(0, len(WITH_Y) * NY * PER)])
    slices = NZ - 1 - len(WITH_Y)
    sent("az", zg.at[pl.ds(0, slices)])
    sent("mw", mwr.at[pl.ds(0, NW - 1)])

    arrived("dy", 0, dyr.at[pl.ds(0, NY - 1)])
    flat = dyr.reshape(NY * YB * SLOTS, 128)
    for s in range(SLOTS):
        rows_s = flat[pl.ds(s, BLKS, stride=SLOTS), :]
        s2[:, pl.ds(s * R, R), :] = rows_s.reshape(CB, R, 128)
    sums = s2[...].reshape(CB * SLOTS * R, 128)
    size = CB * SLOTS * R
    olds = [sf[pl.ds(a * size, size), :] for a in range(3)]
    news = adam(sums * factor, step, *olds)
    slot_row = (lax.broadcasted_iota(jnp.int32, (size, 128), 0) // R) % SLOTS
    live = slot_row.astype(F32) < count
    for a in range(3):
        kept = jnp.where(live, news[a], olds[a]).reshape(CB, SLOTS, R, 128).astype(BF)
        for cb in range(CB):
            nvs[a, :, :, pl.ds(cb * 128, 128)] = kept[cb]
    keep_new = pltpu.make_async_copy(nvs, nv, lsem.at[CB + 1])
    keep_new.start()

    z_wait("mz", mzr)
    peakv[...] = jnp.max(mzr[...], axis=0) + PEAK_EPS
    keep_peak = pltpu.make_async_copy(peakv, peak_ref, lsem.at[CB + 2])
    keep_peak.start()
    sent("dy", dys.at[pl.ds(0, NY - 1)])
    sent("mz", mzr.at[pl.ds(0, NZ - 1)])
    keep_new.wait()
    keep_peak.wait()
    pltpu.make_async_copy(zg.at[pl.ds(0, slices)], zg.at[pl.ds(0, slices)], lsem.at[CB + 3]).wait()
    arrived("ac", 0, tv.at[pl.ds(0, len(WITH_Y) * NY * PER)])
    arrived("ay", 0, tv.at[pl.ds(0, (NY - 1) * slices * PER)])
    sent("ay", tv.at[pl.ds(0, (NY - 1) * slices * PER)])


def finish(
    agb, nv, peak_ref, nw_ref, nm_ref, nv_ref, quant_ref, scale_ref, peakv, nvv, tv, fs, ov, sem
):
    outs = (nw_ref, nm_ref, nv_ref)

    def o_copy(a):
        return pltpu.make_async_copy(nvv.at[a], outs[a], sem.at[CB])

    def t_copy(cb):
        rows = pl.ds(cb * R * 128, R * 128)
        return pltpu.make_async_copy(agb.at[rows], tv.at[rows], sem.at[cb])

    def q_copy(cb):
        return pltpu.make_async_copy(
            ov.at[cb], quant_ref.at[:, :, pl.ds(cb * 128, 128)], sem.at[CB + 1]
        )

    peak_copy = pltpu.make_async_copy(peak_ref, peakv, sem.at[CB + 2])
    peak_copy.start()
    for cb in range(CB):
        t_copy(cb).start()
    nv_copy = pltpu.make_async_copy(nv, nvv, sem.at[CB])
    nv_copy.start()
    peak_copy.wait()
    keep_peak = pltpu.make_async_copy(peakv, scale_ref, sem.at[CB + 2])
    keep_peak.start()
    inverse = jnp.broadcast_to(1.0 / peakv[...], (NT, NT)).T
    o2 = ov.reshape(CB, NT * R, 128)
    for cb in range(CB):
        t_copy(cb).wait()
        for r in range(R):
            block = tv[pl.ds((cb * R + r) * 128, 128), :].T
            fs[pl.ds(r, NT, stride=R), :] = block.astype(F32) * inverse
        o2[cb] = fs[...].astype(BF)
        q_copy(cb).start()
        if cb == 0:
            nv_copy.wait()
            for a in range(3):
                o_copy(a).start()
    keep_peak.wait()
    pltpu.make_async_copy(nvv, nvv, sem.at[CB]).wait()
    pltpu.make_async_copy(ov, ov, sem.at[CB + 1]).wait()


def local(grad_values, grad_scales, owner_ids, step_count, master, moment1, moment2):
    hbm = pl.BlockSpec(memory_space=pltpu.HBM)
    owned = jax.ShapeDtypeStruct((SLOTS, R, COLS), BF)
    V = pltpu.VMEM
    one = V((1, 128), F32)
    exchange = [one, V((NW, 1, 128), F32), one, V((NZ, 1, 128), F32)]
    agb, news, peaks = pl.pallas_call(
        kernel,
        out_shape=(
            jax.ShapeDtypeStruct((NY, NZ, PER, NT), BF),
            jax.ShapeDtypeStruct((3, SLOTS, R, COLS), BF),
            jax.ShapeDtypeStruct((1, NT), F32),
        ),
        in_specs=[hbm] * 7,
        out_specs=(hbm, hbm, hbm),
        scratch_shapes=[
            V((CB, NT, R, 128), BF),
            V((1, NT), F32),
            V((1, NT), jnp.int32),
            V((1, 1), jnp.int32),
            V((1, NT), F32),
            V((NT * R, 128), F32),
            V((E, NT), BF),
            V((3, CB, SLOTS, R, 128), BF),
            V((3 * CB * SLOTS * R, 128), F32),
            V((CB, R * 16, 128), F32),
            V((NY, YB * 16, 128), BF),
            V((NY, YB * 16, 128), BF),
            V((YE, 128), F32),
            V((NZ, 32, 128), BF),
            V((NZ, 32, 128), BF),
            V((len(CLOSE), NY, PER, NT), BF),
            V((NY, PER, NT), F32),
            V((NY, PER, NT), BF),
            V((6 + len(DIRECT), 3, PER, NT), BF),
            V((5 + len(DIRECT), PER, NT), BF),
            V((2, 3, PER, NT), BF),
            V((len(DIRECT) - 1, PER, NT), BF),
            V((128, NT), BF),
            V((NZ, 16, 128), BF),
            V((NZ, 16, 128), BF),
            V((NY, YB * SLOTS, 128), F32),
            V((NY, YB * SLOTS, 128), F32),
            V((CB, SLOTS * R, 128), F32),
            V((3, SLOTS, R, COLS), BF),
        ]
        + exchange
        + exchange
        + [
            V((PER, NT), BF),
            V((NZ, PER, NT), BF),
            V((NY, PER, NT), BF),
            pltpu.SemaphoreType.DMA((CB + 4,)),
            pltpu.SemaphoreType.DMA((len(KINDS),)),
            pltpu.SemaphoreType.DMA((_total,)),
            pltpu.SemaphoreType.REGULAR,
            pltpu.SemaphoreType.REGULAR,
        ],
        compiler_params=pltpu.CompilerParams(
            collective_id=0, has_side_effects=True, vmem_limit_bytes=62 << 20
        ),
        name="exchange",
    )(
        grad_values[0], grad_scales, owner_ids.reshape(1, NT), step_count.reshape(1, 1),
        master[0], moment1[0], moment2[0],
    )
    out = pl.pallas_call(
        finish,
        out_shape=(
            owned, owned, owned,
            jax.ShapeDtypeStruct((NT, R, COLS), BF),
            jax.ShapeDtypeStruct((1, NT), F32),
        ),
        in_specs=[hbm, hbm, hbm],
        out_specs=(hbm,) * 5,
        scratch_shapes=[
            V((1, NT), F32),
            V((3, SLOTS, R, COLS), BF),
            V((E, NT), BF),
            V((NT * R, 128), F32),
            V((CB, NT, R, 128), BF),
            pltpu.SemaphoreType.DMA((CB + 3,)),
        ],
        compiler_params=pltpu.CompilerParams(vmem_limit_bytes=62 << 20),
        name="finish",
    )(agb.reshape(E, NT), news, peaks)
    return out[0][None], out[1][None], out[2][None], out[3], out[4].reshape(NT)


def solution(mesh):
    split = P("dp", None, None, "tensor")
    return jax.shard_map(
        local,
        mesh=mesh,
        in_specs=(split, P("dp", None), P(), P(), split, split, split),
        out_specs=(split, split, split, P(None, None, "tensor"), P()),
        check_vma=False,
    )
```

```python
import jax
import jax.numpy as jnp
from jax import lax
from jax.experimental import pallas as pl
from jax.experimental.pallas import tpu as pltpu
from jax.sharding import PartitionSpec as P

BETA_ONE = 0.9
BETA_TWO = 0.95
RATE = 0.1
DECAY = 0.1
ADAM_EPS = 1e-08
PEAK_EPS = 1e-06
CLIP_RMS = 0.5

NY, NZ, NX, NC = 4, 16, 4, 2
NT, SLOTS, R, COLS = 128, 4, 4, 768
CB = COLS // 128
BLKS = CB * R
E = BLKS * 128
YE = E // NY
PER = YE // NZ
YB = BLKS // NY
MESH = pl.DeviceIdType.MESH
BF, F32 = jnp.bfloat16, jnp.float32

KINDS = ("sy", "sz", "gn", "gy", "gz", "qw", "qz", "dz", "dy", "az", "ay", "an", "ac", "mw", "mz")
SEND = {name: i for i, name in enumerate(KINDS)}
RECV, _total = {}, 0
for _name in KINDS:
    if _name == "az":
        RECV[_name] = RECV["gy"]
        continue
    RECV[_name] = _total
    _total += {"gy": NZ, "gz": 3}.get(_name, 1)
NW = NY * NX * NC
CLOSE = (2, -2, 1, -1)
DIRECT = (8, 3, -3, 4, -4, 0)
WITH_Y = (1, -1)
SPREAD = (4, -4, 8, 2, -2, 3, -3)


def far_offset(j):
    return 8 + (1 - 2 * (j & 1)) * ((j + 1) >> 1)


def relayed(i):
    return 1 - 2 * (i & 1), 7 - (i >> 1)


def adam(g, step, master, first, second):
    m = BETA_ONE * first + (1.0 - BETA_ONE) * g
    v = BETA_TWO * second + (1.0 - BETA_TWO) * g * g
    one = 1.0 - jnp.exp(step * jnp.log(jnp.full_like(step, BETA_ONE)))
    two = 1.0 - jnp.exp(step * jnp.log(jnp.full_like(step, BETA_TWO)))
    m_hat = m / one
    v_hat = v / two
    w = master - RATE * (m_hat / (jnp.sqrt(v_hat) + ADAM_EPS) + DECAY * master)
    return w, m, v


def kernel(
    g_ref, gs_ref, own_ref, step_ref, w_ref, m_ref, v_ref,
    agb, nv, peak_ref,
    gv, gsv, ownv, stepv, peakv, fs, tv, sv, sf, ysf, ys, syr, st, szs, szr,
    nb, close, closeb, yr, zs, rr, zr, sbp, dsend, dr, dys, dyr, s2, nvs,
    qws, qwr, qzs, qzr, mws, mwr, mzs, mzr,
    wown, zg, zn,
    lsem, ssem, rsem, ready, ready_far,
):
    dp, tp = lax.axis_index("dp"), lax.axis_index("tensor")
    y, z = dp >> 4, dp & (NZ - 1)
    w_me = y * (NX * NC) + tp

    def at_z(zz):
        return (y * NZ + zz, tp)

    def at_y(yy):
        return (yy * NZ + z, tp)

    def at_w(k):
        return (((y + (k >> 3)) & (NY - 1)) * NZ + z, (tp + k) & (NX * NC - 1))

    def near(d):
        return (z + d + NZ) & (NZ - 1)

    def send(kind, i, src, dst, dev):
        pltpu.make_async_remote_copy(
            src_ref=src, dst_ref=dst, send_sem=ssem.at[SEND[kind]],
            recv_sem=rsem.at[RECV[kind] + i], device_id=dev, device_id_type=MESH,
        ).start()

    def arrived(kind, i, ref):
        pltpu.make_async_copy(ref, ref, rsem.at[RECV[kind] + i]).wait()

    def sent(kind, ref):
        pltpu.make_async_copy(ref, ref, ssem.at[SEND[kind]]).wait()

    barrier = pltpu.get_barrier_semaphore()

    def greet(device):
        pl.semaphore_signal(barrier, inc=1, device_id=device, device_id_type=MESH)

    for d in (2, -2, 1, -1):
        greet(at_z(near(d)))
    for k in (4, 5, 3, 2, 6, 7, 1):
        greet(at_w(k))
    for k in (2, 1, 3):
        greet(at_y((y + k) & (NY - 1)))

    state = (w_ref, m_ref, v_ref)

    def g_copy(cb):
        return pltpu.make_async_copy(g_ref.at[:, :, pl.ds(cb * 128, 128)], gv.at[cb], lsem.at[cb])

    def s_copy(a, cb):
        return pltpu.make_async_copy(
            state[a].at[:, :, pl.ds(cb * 128, 128)], sv.at[a, cb], lsem.at[CB]
        )

    gs_copy = pltpu.make_async_copy(gs_ref, gsv, lsem.at[CB + 1])
    own_copy = pltpu.make_async_copy(own_ref, ownv, lsem.at[CB + 2])
    gs_copy.start()
    for cb in range(CB):
        g_copy(cb).start()
    own_copy.start()
    step_copy = pltpu.make_async_copy(step_ref, stepv, lsem.at[CB + 3])
    step_copy.start()
    for a in range(3):
        for cb in range(CB):
            s_copy(a, cb).start()

    gs_copy.wait()
    scales = jnp.broadcast_to(gsv[...], (NT, NT)).T
    g2 = gv.reshape(CB, NT * R, 128)
    for cb in range(CB):
        g_copy(cb).wait()
        fs[...] = g2[cb].astype(F32)
        for r in range(R):
            block = fs[pl.ds(r, NT, stride=R), :]
            tv[pl.ds((cb * R + r) * 128, 128), :] = (block * scales).astype(BF).T

    pltpu.make_async_copy(sv, sv, lsem.at[CB]).wait()
    sf[...] = sv.reshape(3 * CB * SLOTS * R, 128)[...].astype(F32)
    ysf[...] = jnp.zeros_like(ysf)
    for a in range(3):
        for r in range(R):
            rows = sf[pl.ds(a * CB * SLOTS * R + r, CB * SLOTS, stride=R), :]
            ysf[:, pl.ds(r * 16 + a * 4, 4), :] = rows.reshape(CB, SLOTS, 128)
    ys[...] = ysf[...].reshape(NY, YB * 16, 128).astype(BF)

    pl.semaphore_wait(barrier, 4 + (NX * NC - 1) + (NY - 1))

    tv4 = tv.reshape(NY, NZ, PER, NT)
    for i, d in enumerate(CLOSE):
        send("gn", 0, tv4.at[:, near(d)], nb.at[i], at_z(near(d)))

    def slice_at(ref, yy, zz):
        return ref.at[pl.ds(pl.multiple_of((yy * NZ + zz) * PER, 16), PER)]

    def y_send(i, zz):
        for k in (1, 3, 2):
            yy = (y + k) & (NY - 1)
            send("gy", i, slice_at(tv, yy, zz), yr.at[i, k - 1], at_y(yy))

    def y_send_relayed(i, carry):
        side, far = relayed(i)
        y_send(i, near(side * far))
        return carry

    lax.fori_loop(0, 6, y_send_relayed, 0)
    for i, d in enumerate(DIRECT[:-1]):
        y_send(6 + i, near(d))

    for k in range(1, NY):
        yy = (y + k) & (NY - 1)
        send("sy", 0, ys.at[yy], syr.at[y], at_y(yy))
    syr[y] = ys[y]

    def tell(sem, hops):
        for d in (hops, -hops):
            pl.semaphore_signal(sem, inc=1, device_id=at_z(near(d)), device_id_type=MESH)

    tell(ready, 2)

    def y_sum(i, total):
        arrived("gy", i, yr.at[i])
        for k in range(3):
            total = total + yr[i, k].astype(F32)
        return total

    def part_of(zz):
        return slice_at(tv, y, zz)[...].astype(F32)

    def to_relay(i, carry):
        side, far = relayed(i)
        zs[i] = y_sum(i, part_of(near(side * far))).astype(BF)
        send("gz", 1 + (i & 1), zs.at[i], rr.at[i & 1, i >> 1], at_z(near(side * (far - 4))))
        return carry

    pl.semaphore_wait(ready, 2)
    tell(ready_far, 4)
    lax.fori_loop(0, 4, to_relay, 0)

    arrived("gn", 0, nb)
    for yy in range(NY):
        total = tv4[yy, z].astype(F32)
        for i in range(len(CLOSE)):
            total = total + nb[i, yy].astype(F32)
        close[yy] = total
        closeb[yy] = total.astype(BF)
    last = 6 + len(DIRECT) - 1
    for k in (1, 3, 2):
        yy = (y + k) & (NY - 1)
        send("gy", last, closeb.at[yy], yr.at[last, k - 1], at_y(yy))

    lax.fori_loop(4, 6, to_relay, 0)
    pl.semaphore_wait(ready_far, 2)
    for i, d in enumerate(DIRECT[:-1]):
        total = y_sum(6 + i, part_of(near(d)))
        if abs(d) == 4:
            side = 0 if d > 0 else 1
            arrived("gz", 1 + side, rr.at[side])
            for k in range(3):
                total = total + rr[side, k].astype(F32)
        zs[6 + i] = total.astype(BF)
        send("gz", 0, zs.at[6 + i], zr.at[i], at_z(near(d)))
    mine = y_sum(last, close[y])

    arrived("sy", 0, syr.at[pl.ds(0, NY - 1)])
    for b in range(YB):
        block = syr[:, pl.ds(b * 16, 16), :].reshape(NY * 16, 128).astype(F32)
        block = jnp.concatenate([block, jnp.zeros((128 - NY * 16, 128), F32)], axis=0)
        st[pl.ds(b * 128, 128), :] = block.T
    for zz in range(NZ):
        upper = st[pl.ds(zz * PER, 16), :] + pltpu.roll(st[pl.ds(zz * PER + 16, 16), :], 64, 1)
        szs[zz, pl.ds(0, 16), :] = upper.astype(BF)
        szs[zz, pl.ds(16, 16), :] = st[pl.ds(zz * PER + 32, 16), :].astype(BF)

    own_copy.wait()
    step_copy.wait()
    own = ownv[...]
    spread = jnp.broadcast_to(own.astype(F32), (NT, NT))
    same = spread == spread.T
    before = lax.broadcasted_iota(jnp.int32, (NT, NT), 0) < lax.broadcasted_iota(jnp.int32, (NT, NT), 1)
    slot = jnp.sum(jnp.where(same & before, 1.0, 0.0), axis=0, keepdims=True).astype(jnp.int32)
    own_z, own_y = own & (NZ - 1), own >> 4
    count = jnp.sum(jnp.where(own == dp, 1.0, 0.0), axis=1, keepdims=True)
    place = own_z * 16 + own_y * 4 + slot
    hot = jnp.where(
        lax.broadcasted_iota(jnp.int32, (NZ * 16, NT), 0) == place, 1.0, 0.0
    ).astype(BF)

    arrived("gz", 0, zr)
    summed = mine
    for i in range(len(DIRECT) - 1):
        summed = summed + zr[i].astype(F32)

    def w_stage(kind, value, sendbuf, buf):
        sendbuf[...] = value
        buf[w_me] = value

        def body(i, carry):
            send(kind, 0, sendbuf, buf.at[w_me], at_w(NW - 1 - i))
            return carry

        lax.fori_loop(0, NW - 1, body, 0)

    def w_wait(kind, buf):
        arrived(kind, 0, buf.at[pl.ds(0, NW - 1)])

    def z_stage(kind, value, sendbuf, buf):
        sendbuf[...] = value
        buf[z] = value

        def body(j, carry):
            send(kind, 0, sendbuf, buf.at[z], at_z(near(far_offset(j))))
            return carry

        lax.fori_loop(0, NZ - 1, body, 0)

    def z_wait(kind, buf):
        arrived(kind, 0, buf.at[pl.ds(0, NZ - 1)])

    squares = jnp.sum(summed * summed, axis=0, keepdims=True)
    w_stage("qw", squares, qws, qwr)

    def sz_send(j, carry):
        zz = near(far_offset(j))
        send("sz", 0, szs.at[zz], szr.at[z], at_z(zz))
        return carry

    lax.fori_loop(0, NZ - 1, sz_send, 0)
    szr[z] = szs[z]

    sum_bf = summed.astype(BF)
    sbp[...] = jnp.zeros_like(sbp)
    sbp[pl.ds(0, PER), :] = sum_bf
    dsend[...] = (
        lax.dot_general(hot, sbp[...], (((1,), (1,)), ((), ())), preferred_element_type=F32)
        .astype(BF)
        .reshape(NZ, 16, 128)
    )
    sent("sy", syr.at[pl.ds(0, NY - 1)])
    sent("gn", nb)
    sent("gy", yr)
    sent("gz", zs)

    w_wait("qw", qwr)
    z_stage("qz", jnp.sum(qwr[...], axis=0), qzs, qzr)

    def d_send(j, carry):
        zz = near(far_offset(j))
        send("dz", 0, dsend.at[zz], dr.at[z], at_z(zz))
        return carry

    lax.fori_loop(0, NZ - 1, d_send, 0)
    dr[z] = dsend[z]

    z_wait("sz", szr)
    low = lax.broadcasted_iota(jnp.int32, (16, 128), 1) < 64
    parts = [[], [], []]
    for pair in range(NZ // 2):
        even0, even1 = szr[2 * pair, pl.ds(0, 16), :].astype(F32), szr[2 * pair, pl.ds(16, 16), :].astype(F32)
        odd0, odd1 = szr[2 * pair + 1, pl.ds(0, 16), :].astype(F32), szr[2 * pair + 1, pl.ds(16, 16), :].astype(F32)
        parts[0].append(jnp.where(low, even0, pltpu.roll(odd0, 64, 1)))
        parts[1].append(jnp.where(low, pltpu.roll(even0, 64, 1), odd0))
        parts[2].append(jnp.where(low, even1, pltpu.roll(odd1, 64, 1)))
    packed = jnp.concatenate([jnp.concatenate(p, axis=1) for p in parts], axis=0).astype(BF)
    target = own_z * 64 + own_y * 16 + slot
    rows = lax.broadcasted_iota(jnp.int32, (NZ * 64, NT), 0)
    old = []
    for a in range(3):
        pick = jnp.where(rows == target + 4 * a, 1.0, 0.0).astype(BF)
        old.append(jnp.dot(packed, pick, preferred_element_type=F32))
    sent("qw", qwr.at[pl.ds(0, NW - 1)])
    sent("sz", szs.at[pl.ds(0, NZ - 1)])

    z_wait("qz", qzr)
    all_squares = jnp.sum(jnp.sum(qzr[...], axis=0), axis=(0, 1), keepdims=True)
    entries = float(NT * R * COLS * NX * NC)
    factor = jnp.minimum(
        1.0, CLIP_RMS * jnp.sqrt(jnp.full((1, 1), entries, F32)) / jnp.sqrt(all_squares + 1e-06)
    )
    step = stepv[...].astype(F32)

    new_w, _, _ = adam(sum_bf.astype(F32) * factor, step, old[0], old[1], old[2])
    new_w = new_w.astype(BF)
    wown[...] = new_w
    zn[y] = new_w

    for d in SPREAD:
        send("az", d % NZ, wown, zg.at[z], at_z(near(d)))
    peak = jnp.max(jnp.abs(new_w.astype(F32)), axis=0, keepdims=True)
    w_stage("mw", peak, mws, mwr)
    for k in (2, 1, 3):
        send("an", 0, wown, zn.at[y], at_y((y + k) & (NY - 1)))

    def take(d):
        zz = near(-d)
        arrived("az", d % NZ, zg.at[zz])
        pltpu.make_async_copy(zg.at[zz], agb.at[y, zz], lsem.at[CB + 3]).start()

    def pass_z(d):
        side = 1 if d > 0 else -1
        for s in (3, 2, 1):
            send("az", (d + side * s) % NZ, zg.at[near(-d)], zg.at[near(-d)], at_z(near(side * s)))

    def pass_y(d):
        zz = near(-d)
        for k in (2, 1, 3):
            send("ay", 0, zg.at[zz], agb.at[y, zz], at_y((y + k) & (NY - 1)))

    arrived("an", 0, zn.at[pl.ds(0, NY - 1)])
    for d in WITH_Y:
        send("ac", 0, zn, agb.at[:, z], at_z(near(d)))
    keep_own = pltpu.make_async_copy(zn, agb.at[:, z], lsem.at[CB + 1])
    keep_own.start()
    for d in (2, -2):
        take(d)
        pass_y(d)
    for d in (4, -4):
        take(d)
        pass_z(d)
    for d in (3, -3):
        take(d)
        pass_y(d)
    for d in (4, -4):
        pass_y(d)

    z_wait("dz", dr)
    lane = lax.broadcasted_iota(jnp.int32, (16, 128), 1)
    for b in range(YB):
        block = jnp.zeros((16, 128), F32)
        for zz in range(NZ):
            start = zz * PER - b * 128
            if -PER < start < 128:
                piece = dr[zz].astype(F32)
                if start % 128:
                    piece = pltpu.roll(piece, start % 128, 1)
                if start < 0:
                    piece = jnp.where(lane < start + PER, piece, 0.0)
                elif start + PER > 128:
                    piece = jnp.where(lane >= start, piece, 0.0)
                block = block + piece
        dys[:, pl.ds(b * 4, 4), :] = block.reshape(NY, SLOTS, 128)
    for k in (2, 1, 3):
        yy = (y + k) & (NY - 1)
        send("dy", 0, dys.at[yy], dyr.at[y], at_y(yy))
    dyr[y] = dys[y]

    w_wait("mw", mwr)
    z_stage("mz", jnp.max(mwr[...], axis=0), mzs, mzr)
    for d in (5, -5, 8, 6, -6, 7, -7):
        take(d)
        pass_y(d)
    sent("qz", qzr.at[pl.ds(0, NZ - 1)])
    sent("dz", dsend.at[pl.ds(0, NZ - 1)])
    keep_own.wait()
    sent("an", zg.at[pl.ds(0, NY - 1)])
    sent("ac", tv.at[pl.ds(0, len(WITH_Y) * NY * PER)])
    slices = NZ - 1 - len(WITH_Y)
    sent("az", zg.at[pl.ds(0, slices)])
    sent("mw", mwr.at[pl.ds(0, NW - 1)])

    arrived("dy", 0, dyr.at[pl.ds(0, NY - 1)])
    flat = dyr.reshape(NY * YB * SLOTS, 128)
    for s in range(SLOTS):
        rows_s = flat[pl.ds(s, BLKS, stride=SLOTS), :]
        s2[:, pl.ds(s * R, R), :] = rows_s.reshape(CB, R, 128)
    sums = s2[...].reshape(CB * SLOTS * R, 128)
    size = CB * SLOTS * R
    olds = [sf[pl.ds(a * size, size), :] for a in range(3)]
    news = adam(sums * factor, step, *olds)
    slot_row = (lax.broadcasted_iota(jnp.int32, (size, 128), 0) // R) % SLOTS
    live = slot_row.astype(F32) < count
    for a in range(3):
        kept = jnp.where(live, news[a], olds[a]).reshape(CB, SLOTS, R, 128).astype(BF)
        for cb in range(CB):
            nvs[a, :, :, pl.ds(cb * 128, 128)] = kept[cb]
    keep_new = pltpu.make_async_copy(nvs, nv, lsem.at[CB + 1])
    keep_new.start()

    z_wait("mz", mzr)
    peakv[...] = jnp.max(mzr[...], axis=0) + PEAK_EPS
    keep_peak = pltpu.make_async_copy(peakv, peak_ref, lsem.at[CB + 2])
    keep_peak.start()
    sent("dy", dys.at[pl.ds(0, NY - 1)])
    sent("mz", mzr.at[pl.ds(0, NZ - 1)])
    keep_new.wait()
    keep_peak.wait()
    pltpu.make_async_copy(zg.at[pl.ds(0, slices)], zg.at[pl.ds(0, slices)], lsem.at[CB + 3]).wait()
    arrived("ac", 0, tv.at[pl.ds(0, len(WITH_Y) * NY * PER)])
    arrived("ay", 0, tv.at[pl.ds(0, (NY - 1) * slices * PER)])
    sent("ay", tv.at[pl.ds(0, (NY - 1) * slices * PER)])


def finish(
    agb, nv, peak_ref, nw_ref, nm_ref, nv_ref, quant_ref, scale_ref, peakv, nvv, tv, fs, ov, sem
):
    outs = (nw_ref, nm_ref, nv_ref)

    def o_copy(a):
        return pltpu.make_async_copy(nvv.at[a], outs[a], sem.at[CB])

    def t_copy(cb):
        rows = pl.ds(cb * R * 128, R * 128)
        return pltpu.make_async_copy(agb.at[rows], tv.at[rows], sem.at[cb])

    def q_copy(cb):
        return pltpu.make_async_copy(
            ov.at[cb], quant_ref.at[:, :, pl.ds(cb * 128, 128)], sem.at[CB + 1]
        )

    peak_copy = pltpu.make_async_copy(peak_ref, peakv, sem.at[CB + 2])
    peak_copy.start()
    for cb in range(CB):
        t_copy(cb).start()
    nv_copy = pltpu.make_async_copy(nv, nvv, sem.at[CB])
    nv_copy.start()
    peak_copy.wait()
    keep_peak = pltpu.make_async_copy(peakv, scale_ref, sem.at[CB + 2])
    keep_peak.start()
    inverse = jnp.broadcast_to(1.0 / peakv[...], (NT, NT)).T
    o2 = ov.reshape(CB, NT * R, 128)
    for cb in range(CB):
        t_copy(cb).wait()
        for r in range(R):
            block = tv[pl.ds((cb * R + r) * 128, 128), :].T
            fs[pl.ds(r, NT, stride=R), :] = block.astype(F32) * inverse
        o2[cb] = fs[...].astype(BF)
        q_copy(cb).start()
        if cb == 0:
            nv_copy.wait()
            for a in range(3):
                o_copy(a).start()
    keep_peak.wait()
    pltpu.make_async_copy(nvv, nvv, sem.at[CB]).wait()
    pltpu.make_async_copy(ov, ov, sem.at[CB + 1]).wait()


def local(grad_values, grad_scales, owner_ids, step_count, master, moment1, moment2):
    hbm = pl.BlockSpec(memory_space=pltpu.HBM)
    owned = jax.ShapeDtypeStruct((SLOTS, R, COLS), BF)
    V = pltpu.VMEM
    one = V((1, 128), F32)
    exchange = [one, V((NW, 1, 128), F32), one, V((NZ, 1, 128), F32)]
    agb, news, peaks = pl.pallas_call(
        kernel,
        out_shape=(
            jax.ShapeDtypeStruct((NY, NZ, PER, NT), BF),
            jax.ShapeDtypeStruct((3, SLOTS, R, COLS), BF),
            jax.ShapeDtypeStruct((1, NT), F32),
        ),
        in_specs=[hbm] * 7,
        out_specs=(hbm, hbm, hbm),
        scratch_shapes=[
            V((CB, NT, R, 128), BF),
            V((1, NT), F32),
            V((1, NT), jnp.int32),
            V((1, 1), jnp.int32),
            V((1, NT), F32),
            V((NT * R, 128), F32),
            V((E, NT), BF),
            V((3, CB, SLOTS, R, 128), BF),
            V((3 * CB * SLOTS * R, 128), F32),
            V((CB, R * 16, 128), F32),
            V((NY, YB * 16, 128), BF),
            V((NY, YB * 16, 128), BF),
            V((YE, 128), F32),
            V((NZ, 32, 128), BF),
            V((NZ, 32, 128), BF),
            V((len(CLOSE), NY, PER, NT), BF),
            V((NY, PER, NT), F32),
            V((NY, PER, NT), BF),
            V((6 + len(DIRECT), 3, PER, NT), BF),
            V((5 + len(DIRECT), PER, NT), BF),
            V((2, 3, PER, NT), BF),
            V((len(DIRECT) - 1, PER, NT), BF),
            V((128, NT), BF),
            V((NZ, 16, 128), BF),
            V((NZ, 16, 128), BF),
            V((NY, YB * SLOTS, 128), F32),
            V((NY, YB * SLOTS, 128), F32),
            V((CB, SLOTS * R, 128), F32),
            V((3, SLOTS, R, COLS), BF),
        ]
        + exchange
        + exchange
        + [
            V((PER, NT), BF),
            V((NZ, PER, NT), BF),
            V((NY, PER, NT), BF),
            pltpu.SemaphoreType.DMA((CB + 4,)),
            pltpu.SemaphoreType.DMA((len(KINDS),)),
            pltpu.SemaphoreType.DMA((_total,)),
            pltpu.SemaphoreType.REGULAR,
            pltpu.SemaphoreType.REGULAR,
        ],
        compiler_params=pltpu.CompilerParams(
            collective_id=0, has_side_effects=True, vmem_limit_bytes=62 << 20
        ),
        name="exchange",
    )(
        grad_values[0], grad_scales, owner_ids.reshape(1, NT), step_count.reshape(1, 1),
        master[0], moment1[0], moment2[0],
    )
    out = pl.pallas_call(
        finish,
        out_shape=(
            owned, owned, owned,
            jax.ShapeDtypeStruct((NT, R, COLS), BF),
            jax.ShapeDtypeStruct((1, NT), F32),
        ),
        in_specs=[hbm, hbm, hbm],
        out_specs=(hbm,) * 5,
        scratch_shapes=[
            V((1, NT), F32),
            V((3, SLOTS, R, COLS), BF),
            V((E, NT), BF),
            V((NT * R, 128), F32),
            V((CB, NT, R, 128), BF),
            pltpu.SemaphoreType.DMA((CB + 3,)),
        ],
        compiler_params=pltpu.CompilerParams(vmem_limit_bytes=62 << 20),
        name="finish",
    )(agb.reshape(E, NT), news, peaks)
    return out[0][None], out[1][None], out[2][None], out[3], out[4].reshape(NT)


def solution(mesh):
    split = P("dp", None, None, "tensor")
    return jax.shard_map(
        local,
        mesh=mesh,
        in_specs=(split, P("dp", None), P(), P(), split, split, split),
        out_specs=(split, split, split, P(None, None, "tensor"), P()),
        check_vma=False,
    )
```

```python
import jax
import jax.numpy as jnp
from jax import lax
from jax.experimental import pallas as pl
from jax.experimental.pallas import tpu as pltpu
from jax.sharding import PartitionSpec as P

BETA_ONE = 0.9
BETA_TWO = 0.95
RATE = 0.1
DECAY = 0.1
ADAM_EPS = 1e-08
PEAK_EPS = 1e-06
CLIP_RMS = 0.5

NY, NZ, NX, NC = 4, 16, 4, 2
NT, SLOTS, R, COLS = 128, 4, 4, 768
CB = COLS // 128
BLKS = CB * R
E = BLKS * 128
YE = E // NY
PER = YE // NZ
YB = BLKS // NY
MESH = pl.DeviceIdType.MESH
BF, F32 = jnp.bfloat16, jnp.float32

KINDS = ("sy", "sz", "gn", "gy", "gz", "qw", "qz", "dz", "dy", "az", "ay", "an", "ac", "mw", "mz")
SEND = {name: i for i, name in enumerate(KINDS)}
RECV, _total = {}, 0
for _name in KINDS:
    if _name == "az":
        RECV[_name] = RECV["gy"]
        continue
    RECV[_name] = _total
    _total += {"gy": NZ, "gz": 3}.get(_name, 1)
NW = NY * NX * NC
CLOSE = (2, -2, 1, -1)
DIRECT = (8, 3, -3, 4, -4, 0)
WITH_Y = (1, -1)
SPREAD = (4, -4, 8, 2, -2, 3, -3)


def far_offset(j):
    return 8 + (1 - 2 * (j & 1)) * ((j + 1) >> 1)


def relayed(i):
    return 1 - 2 * (i & 1), 7 - (i >> 1)


def adam(g, step, master, first, second):
    m = BETA_ONE * first + (1.0 - BETA_ONE) * g
    v = BETA_TWO * second + (1.0 - BETA_TWO) * g * g
    one = 1.0 - jnp.exp(step * jnp.log(jnp.full_like(step, BETA_ONE)))
    two = 1.0 - jnp.exp(step * jnp.log(jnp.full_like(step, BETA_TWO)))
    m_hat = m / one
    v_hat = v / two
    w = master - RATE * (m_hat / (jnp.sqrt(v_hat) + ADAM_EPS) + DECAY * master)
    return w, m, v


def kernel(
    g_ref, gs_ref, own_ref, step_ref, w_ref, m_ref, v_ref,
    agb, nv, peak_ref,
    gv, gsv, ownv, stepv, peakv, fs, tv, sv, sf, ysf, ys, syr, st, szs, szr,
    nb, close, closeb, yr, zs, rr, zr, sbp, dsend, dr, dys, dyr, s2, nvs,
    qws, qwr, qzs, qzr, mws, mwr, mzs, mzr,
    wown, zg, zn,
    lsem, ssem, rsem, ready, ready_far,
):
    dp, tp = lax.axis_index("dp"), lax.axis_index("tensor")
    y, z = dp >> 4, dp & (NZ - 1)
    w_me = y * (NX * NC) + tp

    def at_z(zz):
        return (y * NZ + zz, tp)

    def at_y(yy):
        return (yy * NZ + z, tp)

    def at_w(k):
        return (((y + (k >> 3)) & (NY - 1)) * NZ + z, (tp + k) & (NX * NC - 1))

    def near(d):
        return (z + d + NZ) & (NZ - 1)

    def send(kind, i, src, dst, dev):
        pltpu.make_async_remote_copy(
            src_ref=src, dst_ref=dst, send_sem=ssem.at[SEND[kind]],
            recv_sem=rsem.at[RECV[kind] + i], device_id=dev, device_id_type=MESH,
        ).start()

    def arrived(kind, i, ref):
        pltpu.make_async_copy(ref, ref, rsem.at[RECV[kind] + i]).wait()

    def sent(kind, ref):
        pltpu.make_async_copy(ref, ref, ssem.at[SEND[kind]]).wait()

    barrier = pltpu.get_barrier_semaphore()

    def greet(device):
        pl.semaphore_signal(barrier, inc=1, device_id=device, device_id_type=MESH)

    for d in (2, -2, 1, -1):
        greet(at_z(near(d)))
    for k in (4, 5, 3, 2, 6, 7, 1):
        greet(at_w(k))
    for k in (2, 1, 3):
        greet(at_y((y + k) & (NY - 1)))

    state = (w_ref, m_ref, v_ref)

    def g_copy(cb):
        return pltpu.make_async_copy(g_ref.at[:, :, pl.ds(cb * 128, 128)], gv.at[cb], lsem.at[cb])

    def s_copy(a, cb):
        return pltpu.make_async_copy(
            state[a].at[:, :, pl.ds(cb * 128, 128)], sv.at[a, cb], lsem.at[CB]
        )

    gs_copy = pltpu.make_async_copy(gs_ref, gsv, lsem.at[CB + 1])
    own_copy = pltpu.make_async_copy(own_ref, ownv, lsem.at[CB + 2])
    gs_copy.start()
    for cb in range(CB):
        g_copy(cb).start()
    own_copy.start()
    step_copy = pltpu.make_async_copy(step_ref, stepv, lsem.at[CB + 3])
    step_copy.start()
    for a in range(3):
        for cb in range(CB):
            s_copy(a, cb).start()

    gs_copy.wait()
    scales = jnp.broadcast_to(gsv[...], (NT, NT)).T
    g2 = gv.reshape(CB, NT * R, 128)
    for cb in range(CB):
        g_copy(cb).wait()
        fs[...] = g2[cb].astype(F32)
        for r in range(R):
            block = fs[pl.ds(r, NT, stride=R), :]
            tv[pl.ds((cb * R + r) * 128, 128), :] = (block * scales).astype(BF).T

    pltpu.make_async_copy(sv, sv, lsem.at[CB]).wait()
    sf[...] = sv.reshape(3 * CB * SLOTS * R, 128)[...].astype(F32)
    ysf[...] = jnp.zeros_like(ysf)
    for a in range(3):
        for r in range(R):
            rows = sf[pl.ds(a * CB * SLOTS * R + r, CB * SLOTS, stride=R), :]
            ysf[:, pl.ds(r * 16 + a * 4, 4), :] = rows.reshape(CB, SLOTS, 128)
    ys[...] = ysf[...].reshape(NY, YB * 16, 128).astype(BF)

    pl.semaphore_wait(barrier, 4 + (NX * NC - 1) + (NY - 1))

    tv4 = tv.reshape(NY, NZ, PER, NT)
    for i, d in enumerate(CLOSE):
        send("gn", 0, tv4.at[:, near(d)], nb.at[i], at_z(near(d)))

    def slice_at(ref, yy, zz):
        return ref.at[pl.ds(pl.multiple_of((yy * NZ + zz) * PER, 16), PER)]

    def y_send(i, zz):
        for k in (1, 3, 2):
            yy = (y + k) & (NY - 1)
            send("gy", i, slice_at(tv, yy, zz), yr.at[i, k - 1], at_y(yy))

    def y_send_relayed(i, carry):
        side, far = relayed(i)
        y_send(i, near(side * far))
        return carry

    lax.fori_loop(0, 6, y_send_relayed, 0)
    for i, d in enumerate(DIRECT[:-1]):
        y_send(6 + i, near(d))

    for k in range(1, NY):
        yy = (y + k) & (NY - 1)
        send("sy", 0, ys.at[yy], syr.at[y], at_y(yy))
    syr[y] = ys[y]

    def tell(sem, hops):
        for d in (hops, -hops):
            pl.semaphore_signal(sem, inc=1, device_id=at_z(near(d)), device_id_type=MESH)

    tell(ready, 2)

    def y_sum(i, total):
        arrived("gy", i, yr.at[i])
        for k in range(3):
            total = total + yr[i, k].astype(F32)
        return total

    def part_of(zz):
        return slice_at(tv, y, zz)[...].astype(F32)

    def to_relay(i, carry):
        side, far = relayed(i)
        zs[i] = y_sum(i, part_of(near(side * far))).astype(BF)
        send("gz", 1 + (i & 1), zs.at[i], rr.at[i & 1, i >> 1], at_z(near(side * (far - 4))))
        return carry

    pl.semaphore_wait(ready, 2)
    tell(ready_far, 4)
    lax.fori_loop(0, 6, to_relay, 0)

    arrived("gn", 0, nb)
    for yy in range(NY):
        total = tv4[yy, z].astype(F32)
        for i in range(len(CLOSE)):
            total = total + nb[i, yy].astype(F32)
        close[yy] = total
        closeb[yy] = total.astype(BF)
    last = 6 + len(DIRECT) - 1
    for k in (1, 3, 2):
        yy = (y + k) & (NY - 1)
        send("gy", last, closeb.at[yy], yr.at[last, k - 1], at_y(yy))

    pl.semaphore_wait(ready_far, 2)
    for i, d in enumerate(DIRECT[:-1]):
        total = y_sum(6 + i, part_of(near(d)))
        if abs(d) == 4:
            side = 0 if d > 0 else 1
            arrived("gz", 1 + side, rr.at[side])
            for k in range(3):
                total = total + rr[side, k].astype(F32)
        zs[6 + i] = total.astype(BF)
        send("gz", 0, zs.at[6 + i], zr.at[i], at_z(near(d)))
    mine = y_sum(last, close[y])

    arrived("sy", 0, syr.at[pl.ds(0, NY - 1)])
    for b in range(YB):
        block = syr[:, pl.ds(b * 16, 16), :].reshape(NY * 16, 128).astype(F32)
        block = jnp.concatenate([block, jnp.zeros((128 - NY * 16, 128), F32)], axis=0)
        st[pl.ds(b * 128, 128), :] = block.T
    for zz in range(NZ):
        upper = st[pl.ds(zz * PER, 16), :] + pltpu.roll(st[pl.ds(zz * PER + 16, 16), :], 64, 1)
        szs[zz, pl.ds(0, 16), :] = upper.astype(BF)
        szs[zz, pl.ds(16, 16), :] = st[pl.ds(zz * PER + 32, 16), :].astype(BF)

    own_copy.wait()
    step_copy.wait()
    own = ownv[...]
    spread = jnp.broadcast_to(own.astype(F32), (NT, NT))
    same = spread == spread.T
    before = lax.broadcasted_iota(jnp.int32, (NT, NT), 0) < lax.broadcasted_iota(jnp.int32, (NT, NT), 1)
    slot = jnp.sum(jnp.where(same & before, 1.0, 0.0), axis=0, keepdims=True).astype(jnp.int32)
    own_z, own_y = own & (NZ - 1), own >> 4
    count = jnp.sum(jnp.where(own == dp, 1.0, 0.0), axis=1, keepdims=True)
    place = own_z * 16 + own_y * 4 + slot
    hot = jnp.where(
        lax.broadcasted_iota(jnp.int32, (NZ * 16, NT), 0) == place, 1.0, 0.0
    ).astype(BF)

    arrived("gz", 0, zr)
    summed = mine
    for i in range(len(DIRECT) - 1):
        summed = summed + zr[i].astype(F32)

    def w_stage(kind, value, sendbuf, buf):
        sendbuf[...] = value
        buf[w_me] = value

        def body(i, carry):
            send(kind, 0, sendbuf, buf.at[w_me], at_w(NW - 1 - i))
            return carry

        lax.fori_loop(0, NW - 1, body, 0)

    def w_wait(kind, buf):
        arrived(kind, 0, buf.at[pl.ds(0, NW - 1)])

    def z_stage(kind, value, sendbuf, buf):
        sendbuf[...] = value
        buf[z] = value

        def body(j, carry):
            send(kind, 0, sendbuf, buf.at[z], at_z(near(far_offset(j))))
            return carry

        lax.fori_loop(0, NZ - 1, body, 0)

    def z_wait(kind, buf):
        arrived(kind, 0, buf.at[pl.ds(0, NZ - 1)])

    squares = jnp.sum(summed * summed, axis=0, keepdims=True)
    w_stage("qw", squares, qws, qwr)

    def sz_send(j, carry):
        zz = near(far_offset(j))
        send("sz", 0, szs.at[zz], szr.at[z], at_z(zz))
        return carry

    lax.fori_loop(0, NZ - 1, sz_send, 0)
    szr[z] = szs[z]

    sum_bf = summed.astype(BF)
    sbp[...] = jnp.zeros_like(sbp)
    sbp[pl.ds(0, PER), :] = sum_bf
    dsend[...] = (
        lax.dot_general(hot, sbp[...], (((1,), (1,)), ((), ())), preferred_element_type=F32)
        .astype(BF)
        .reshape(NZ, 16, 128)
    )
    sent("sy", syr.at[pl.ds(0, NY - 1)])
    sent("gn", nb)
    sent("gy", yr)
    sent("gz", zs)

    w_wait("qw", qwr)
    z_stage("qz", jnp.sum(qwr[...], axis=0), qzs, qzr)

    def d_send(j, carry):
        zz = near(far_offset(j))
        send("dz", 0, dsend.at[zz], dr.at[z], at_z(zz))
        return carry

    lax.fori_loop(0, NZ - 1, d_send, 0)
    dr[z] = dsend[z]

    z_wait("sz", szr)
    low = lax.broadcasted_iota(jnp.int32, (16, 128), 1) < 64
    parts = [[], [], []]
    for pair in range(NZ // 2):
        even0, even1 = szr[2 * pair, pl.ds(0, 16), :].astype(F32), szr[2 * pair, pl.ds(16, 16), :].astype(F32)
        odd0, odd1 = szr[2 * pair + 1, pl.ds(0, 16), :].astype(F32), szr[2 * pair + 1, pl.ds(16, 16), :].astype(F32)
        parts[0].append(jnp.where(low, even0, pltpu.roll(odd0, 64, 1)))
        parts[1].append(jnp.where(low, pltpu.roll(even0, 64, 1), odd0))
        parts[2].append(jnp.where(low, even1, pltpu.roll(odd1, 64, 1)))
    packed = jnp.concatenate([jnp.concatenate(p, axis=1) for p in parts], axis=0).astype(BF)
    target = own_z * 64 + own_y * 16 + slot
    rows = lax.broadcasted_iota(jnp.int32, (NZ * 64, NT), 0)
    old = []
    for a in range(3):
        pick = jnp.where(rows == target + 4 * a, 1.0, 0.0).astype(BF)
        old.append(jnp.dot(packed, pick, preferred_element_type=F32))
    sent("qw", qwr.at[pl.ds(0, NW - 1)])
    sent("sz", szs.at[pl.ds(0, NZ - 1)])

    z_wait("qz", qzr)
    all_squares = jnp.sum(jnp.sum(qzr[...], axis=0), axis=(0, 1), keepdims=True)
    entries = float(NT * R * COLS * NX * NC)
    factor = jnp.minimum(
        1.0, CLIP_RMS * jnp.sqrt(jnp.full((1, 1), entries, F32)) / jnp.sqrt(all_squares + 1e-06)
    )
    step = stepv[...].astype(F32)

    new_w, _, _ = adam(sum_bf.astype(F32) * factor, step, old[0], old[1], old[2])
    new_w = new_w.astype(BF)
    wown[...] = new_w
    zn[y] = new_w

    for d in SPREAD:
        send("az", d % NZ, wown, zg.at[z], at_z(near(d)))
    peak = jnp.max(jnp.abs(new_w.astype(F32)), axis=0, keepdims=True)
    w_stage("mw", peak, mws, mwr)
    for k in (2, 1, 3):
        send("an", 0, wown, zn.at[y], at_y((y + k) & (NY - 1)))

    def take(d):
        zz = near(-d)
        arrived("az", d % NZ, zg.at[zz])
        pltpu.make_async_copy(zg.at[zz], agb.at[y, zz], lsem.at[CB + 3]).start()

    def pass_z(d):
        side = 1 if d > 0 else -1
        for s in (3, 2, 1):
            send("az", (d + side * s) % NZ, zg.at[near(-d)], zg.at[near(-d)], at_z(near(side * s)))

    def pass_y(d):
        zz = near(-d)
        for k in (2, 1, 3):
            send("ay", 0, zg.at[zz], agb.at[y, zz], at_y((y + k) & (NY - 1)))

    arrived("an", 0, zn.at[pl.ds(0, NY - 1)])
    for d in WITH_Y:
        send("ac", 0, zn, agb.at[:, z], at_z(near(d)))
    keep_own = pltpu.make_async_copy(zn, agb.at[:, z], lsem.at[CB + 1])
    keep_own.start()
    for d in (2, -2):
        take(d)
        pass_y(d)
    for d in (4, -4):
        take(d)
        pass_z(d)
    for d in (3, -3):
        take(d)
        pass_y(d)
    for d in (4, -4):
        pass_y(d)

    z_wait("dz", dr)
    lane = lax.broadcasted_iota(jnp.int32, (16, 128), 1)
    for b in range(YB):
        block = jnp.zeros((16, 128), F32)
        for zz in range(NZ):
            start = zz * PER - b * 128
            if -PER < start < 128:
                piece = dr[zz].astype(F32)
                if start % 128:
                    piece = pltpu.roll(piece, start % 128, 1)
                if start < 0:
                    piece = jnp.where(lane < start + PER, piece, 0.0)
                elif start + PER > 128:
                    piece = jnp.where(lane >= start, piece, 0.0)
                block = block + piece
        dys[:, pl.ds(b * 4, 4), :] = block.reshape(NY, SLOTS, 128)
    for k in (2, 1, 3):
        yy = (y + k) & (NY - 1)
        send("dy", 0, dys.at[yy], dyr.at[y], at_y(yy))
    dyr[y] = dys[y]

    w_wait("mw", mwr)
    z_stage("mz", jnp.max(mwr[...], axis=0), mzs, mzr)
    for d in (5, -5, 8, 6, -6, 7, -7):
        take(d)
        pass_y(d)
    sent("qz", qzr.at[pl.ds(0, NZ - 1)])
    sent("dz", dsend.at[pl.ds(0, NZ - 1)])
    keep_own.wait()
    sent("an", zg.at[pl.ds(0, NY - 1)])
    sent("ac", tv.at[pl.ds(0, len(WITH_Y) * NY * PER)])
    slices = NZ - 1 - len(WITH_Y)
    sent("az", zg.at[pl.ds(0, slices)])
    sent("mw", mwr.at[pl.ds(0, NW - 1)])

    arrived("dy", 0, dyr.at[pl.ds(0, NY - 1)])
    flat = dyr.reshape(NY * YB * SLOTS, 128)
    for s in range(SLOTS):
        rows_s = flat[pl.ds(s, BLKS, stride=SLOTS), :]
        s2[:, pl.ds(s * R, R), :] = rows_s.reshape(CB, R, 128)
    sums = s2[...].reshape(CB * SLOTS * R, 128)
    size = CB * SLOTS * R
    olds = [sf[pl.ds(a * size, size), :] for a in range(3)]
    news = adam(sums * factor, step, *olds)
    slot_row = (lax.broadcasted_iota(jnp.int32, (size, 128), 0) // R) % SLOTS
    live = slot_row.astype(F32) < count
    for a in range(3):
        kept = jnp.where(live, news[a], olds[a]).reshape(CB, SLOTS, R, 128).astype(BF)
        for cb in range(CB):
            nvs[a, :, :, pl.ds(cb * 128, 128)] = kept[cb]
    keep_new = pltpu.make_async_copy(nvs, nv, lsem.at[CB + 1])
    keep_new.start()

    z_wait("mz", mzr)
    peakv[...] = jnp.max(mzr[...], axis=0) + PEAK_EPS
    keep_peak = pltpu.make_async_copy(peakv, peak_ref, lsem.at[CB + 2])
    keep_peak.start()
    sent("dy", dys.at[pl.ds(0, NY - 1)])
    sent("mz", mzr.at[pl.ds(0, NZ - 1)])
    keep_new.wait()
    keep_peak.wait()
    pltpu.make_async_copy(zg.at[pl.ds(0, slices)], zg.at[pl.ds(0, slices)], lsem.at[CB + 3]).wait()
    arrived("ac", 0, tv.at[pl.ds(0, len(WITH_Y) * NY * PER)])
    arrived("ay", 0, tv.at[pl.ds(0, (NY - 1) * slices * PER)])
    sent("ay", tv.at[pl.ds(0, (NY - 1) * slices * PER)])


def finish(
    agb, nv, peak_ref, nw_ref, nm_ref, nv_ref, quant_ref, scale_ref, peakv, nvv, tv, fs, ov, sem
):
    outs = (nw_ref, nm_ref, nv_ref)

    def o_copy(a):
        return pltpu.make_async_copy(nvv.at[a], outs[a], sem.at[CB])

    def t_copy(cb):
        rows = pl.ds(cb * R * 128, R * 128)
        return pltpu.make_async_copy(agb.at[rows], tv.at[rows], sem.at[cb])

    def q_copy(cb):
        return pltpu.make_async_copy(
            ov.at[cb], quant_ref.at[:, :, pl.ds(cb * 128, 128)], sem.at[CB + 1]
        )

    peak_copy = pltpu.make_async_copy(peak_ref, peakv, sem.at[CB + 2])
    peak_copy.start()
    for cb in range(CB):
        t_copy(cb).start()
    nv_copy = pltpu.make_async_copy(nv, nvv, sem.at[CB])
    nv_copy.start()
    peak_copy.wait()
    keep_peak = pltpu.make_async_copy(peakv, scale_ref, sem.at[CB + 2])
    keep_peak.start()
    inverse = jnp.broadcast_to(1.0 / peakv[...], (NT, NT)).T
    o2 = ov.reshape(CB, NT * R, 128)
    for cb in range(CB):
        t_copy(cb).wait()
        for r in range(R):
            block = tv[pl.ds((cb * R + r) * 128, 128), :].T
            fs[pl.ds(r, NT, stride=R), :] = block.astype(F32) * inverse
        o2[cb] = fs[...].astype(BF)
        q_copy(cb).start()
        if cb == 0:
            nv_copy.wait()
            for a in range(3):
                o_copy(a).start()
    keep_peak.wait()
    pltpu.make_async_copy(nvv, nvv, sem.at[CB]).wait()
    pltpu.make_async_copy(ov, ov, sem.at[CB + 1]).wait()


def local(grad_values, grad_scales, owner_ids, step_count, master, moment1, moment2):
    hbm = pl.BlockSpec(memory_space=pltpu.HBM)
    owned = jax.ShapeDtypeStruct((SLOTS, R, COLS), BF)
    V = pltpu.VMEM
    one = V((1, 128), F32)
    exchange = [one, V((NW, 1, 128), F32), one, V((NZ, 1, 128), F32)]
    agb, news, peaks = pl.pallas_call(
        kernel,
        out_shape=(
            jax.ShapeDtypeStruct((NY, NZ, PER, NT), BF),
            jax.ShapeDtypeStruct((3, SLOTS, R, COLS), BF),
            jax.ShapeDtypeStruct((1, NT), F32),
        ),
        in_specs=[hbm] * 7,
        out_specs=(hbm, hbm, hbm),
        scratch_shapes=[
            V((CB, NT, R, 128), BF),
            V((1, NT), F32),
            V((1, NT), jnp.int32),
            V((1, 1), jnp.int32),
            V((1, NT), F32),
            V((NT * R, 128), F32),
            V((E, NT), BF),
            V((3, CB, SLOTS, R, 128), BF),
            V((3 * CB * SLOTS * R, 128), F32),
            V((CB, R * 16, 128), F32),
            V((NY, YB * 16, 128), BF),
            V((NY, YB * 16, 128), BF),
            V((YE, 128), F32),
            V((NZ, 32, 128), BF),
            V((NZ, 32, 128), BF),
            V((len(CLOSE), NY, PER, NT), BF),
            V((NY, PER, NT), F32),
            V((NY, PER, NT), BF),
            V((6 + len(DIRECT), 3, PER, NT), BF),
            V((5 + len(DIRECT), PER, NT), BF),
            V((2, 3, PER, NT), BF),
            V((len(DIRECT) - 1, PER, NT), BF),
            V((128, NT), BF),
            V((NZ, 16, 128), BF),
            V((NZ, 16, 128), BF),
            V((NY, YB * SLOTS, 128), F32),
            V((NY, YB * SLOTS, 128), F32),
            V((CB, SLOTS * R, 128), F32),
            V((3, SLOTS, R, COLS), BF),
        ]
        + exchange
        + exchange
        + [
            V((PER, NT), BF),
            V((NZ, PER, NT), BF),
            V((NY, PER, NT), BF),
            pltpu.SemaphoreType.DMA((CB + 4,)),
            pltpu.SemaphoreType.DMA((len(KINDS),)),
            pltpu.SemaphoreType.DMA((_total,)),
            pltpu.SemaphoreType.REGULAR,
            pltpu.SemaphoreType.REGULAR,
        ],
        compiler_params=pltpu.CompilerParams(
            collective_id=0, has_side_effects=True, vmem_limit_bytes=62 << 20
        ),
        name="exchange",
    )(
        grad_values[0], grad_scales, owner_ids.reshape(1, NT), step_count.reshape(1, 1),
        master[0], moment1[0], moment2[0],
    )
    out = pl.pallas_call(
        finish,
        out_shape=(
            owned, owned, owned,
            jax.ShapeDtypeStruct((NT, R, COLS), BF),
            jax.ShapeDtypeStruct((1, NT), F32),
        ),
        in_specs=[hbm, hbm, hbm],
        out_specs=(hbm,) * 5,
        scratch_shapes=[
            V((1, NT), F32),
            V((3, SLOTS, R, COLS), BF),
            V((E, NT), BF),
            V((NT * R, 128), F32),
            V((CB, NT, R, 128), BF),
            pltpu.SemaphoreType.DMA((CB + 3,)),
        ],
        compiler_params=pltpu.CompilerParams(vmem_limit_bytes=62 << 20),
        name="finish",
    )(agb.reshape(E, NT), news, peaks)
    return out[0][None], out[1][None], out[2][None], out[3], out[4].reshape(NT)


def solution(mesh):
    split = P("dp", None, None, "tensor")
    return jax.shard_map(
        local,
        mesh=mesh,
        in_specs=(split, P("dp", None), P(), P(), split, split, split),
        out_specs=(split, split, split, P(None, None, "tensor"), P()),
        check_vma=False,
    )
```
